32 devices in a mesh: groups: 2 (over y), batch: 16 (over z, x, core).
Axes of the slice: x: 2, y: 2, z: 4, core: 2. Of those that a mesh axis runs over, the one named last changes fastest.
Arguments:
- queries: bfloat16 [64, 34, 8192], P(('groups', 'batch')), parts along dimension 0, may hold values from -6 to 6
- key_vectors: bfloat16 [64, 34, 8192], P(('groups', 'batch')), parts along dimension 0, may hold values from -0.5 to 0.5
- values: bfloat16 [64, 34, 8192], P(('groups', 'batch')), parts along dimension 0, may hold values from -6 to 6
- gate_logits: bfloat16 [64, 34, 8192], P(('groups', 'batch')), parts along dimension 0, may hold values from -6 to 6
- decay_rates: float32 [64], replicated, may hold values from 0.003 to 0.08
- norm_gain: float32 [8192], replicated, may hold values from 0.1 to 1.9
- pool_states: bfloat16 [32, 8192, 128], P(('groups', 'batch')), parts along dimension 0, may hold values from -1.75 to 1.75
- pool_entry: int32 [64], P(('groups', 'batch')), parts along dimension 0, may hold values from 0 to 15
Outputs:
- mixed: bfloat16 [64, 34, 8192], P(('groups', 'batch')), parts along dimension 0
- new_states: bfloat16 [64, 8192, 128], P('groups', 'batch'), parts along dimension 0
The draws below stay inside these ranges and needn't reach their ends.
There are 2 independent parts, one for each index of `groups`. The reference program is written for one: setup_inputs(seed, part) draws one part's arguments, and reference() takes and returns one part's arrays. A program takes and returns all parts, laid end to end along the dimension named above; an argument that names none is the same for every part. Nothing has to cross between parts.
Inputs may be any that keep to these rules, and one draw needn't show every extreme that they name: `pool_entry`: entry e is the only entry of the pool shard on batch device e; several requests may name the same entry.
All inputs are finite; a program needn't handle non-finite values.
Results may differ from the reference program's by a relative error of at most 0.001.
Values may be sent and summed in bfloat16 or wider, within the bound.
A program may use at most 64 MiB of HBM per device.

```python
import math
import jax
import jax.numpy as jnp
import numpy as np
from jax import lax

HEADS = 64
HEAD = 128
REQS = 32
ENTRIES = 16
LEN = 34
WIDTH = 8192


def place_ends(values, own_key, least, largest):
    dims = values.shape
    place = [jax.random.randint(jax.random.fold_in(own_key, axis), (), 0, dims[axis]) for axis in range(len(dims))]
    values = values.at[tuple(place)].set(least)
    longest = dims.index(max(dims))
    place[longest] = (place[longest] + 1) % dims[longest]
    return values.at[tuple(place)].set(largest)


def block_scale(rng, dims, split, low, top_value):
    gain = 1.0
    for axis_at, blocks in split:
        heights = jax.random.uniform(jax.random.fold_in(jax.random.fold_in(rng, 6), axis_at), (blocks,), jnp.float32, low / len(split), top_value / len(split))
        gain = gain * jnp.repeat(jnp.exp(heights), dims[axis_at] // blocks).reshape((-1,) + (1,) * (len(dims) - 1 - axis_at))
    return gain


def cumulative_ranks(count, lean):
    weights = [(1 << 20) // math.isqrt(rank ** lean) + 1 for rank in range(1, count + 1)]
    width = 1 + sum(weights) // (1 << 30)
    return np.cumsum(np.array([max(1, weight // width) for weight in weights]))


def skewed_ids(stream_key, shape, amount, lean):
    listing = cumulative_ranks(amount, lean)
    lot = jax.random.randint(jax.random.fold_in(stream_key, 1), shape, 0, int(listing[amount - 1]))
    standing = jnp.searchsorted(jnp.asarray(listing, jnp.int32), lot, side="right")
    return jax.random.permutation(jax.random.fold_in(stream_key, 2), amount)[standing].astype(jnp.int32)


def normal_values(own_key, shape, scale, limit, pieces=(), kind=jnp.bfloat16):
    gain = block_scale(own_key, shape, pieces, -0.22, 0.18) if pieces else 1.0
    values = jax.random.normal(own_key, shape, jnp.float32) * scale * gain
    return jnp.minimum(jnp.maximum(values, -limit), limit).astype(kind)


def setup_inputs(seed: int = 0, part: int = 0) -> dict:
    key_of = jax.random.split(jax.random.key(seed), 9)
    part_splits = jax.random.split(jax.random.fold_in(key_of[8], part), 9)
    queries = normal_values(part_splits[0], (REQS, LEN, WIDTH), 1.0, 6.0, ((0, 16),))
    key_vectors = normal_values(part_splits[1], (REQS, LEN, WIDTH), (HEAD ** -0.5), 0.5, ((0, 16),))
    values = normal_values(part_splits[2], (REQS, LEN, WIDTH), 1.0, 6.0, ((0, 16),))
    gate_logits = normal_values(part_splits[3], (REQS, LEN, WIDTH), 1.0, 6.0, ((0, 16),))
    decay_rates = jnp.clip(jnp.exp(jax.random.uniform(key_of[4], (HEADS,), jnp.float32, math.log(0.003), math.log(0.08))), 0.003, 0.08)
    norm_gain = jnp.clip(1.0 + 0.18 * jax.random.normal(key_of[5], (WIDTH,), jnp.float32), 0.1, 1.9)
    pool_states = normal_values(part_splits[6], (ENTRIES, WIDTH, HEAD), 0.3, 1.75, ((0, 16),))
    pool_entry = place_ends(skewed_ids(part_splits[7], (REQS,), ENTRIES, 2), jax.random.fold_in(part_splits[7], 3), 0, ENTRIES - 1).astype(jnp.int32)
    return dict(queries=queries, key_vectors=key_vectors, values=values, gate_logits=gate_logits, decay_rates=decay_rates, norm_gain=norm_gain, pool_states=pool_states, pool_entry=pool_entry)


def finish_output(attended, gate_logits, norm_gain):
    mean_square = lax.optimization_barrier(jnp.mean(attended * attended, axis=-1, keepdims=True))
    scaled = attended * lax.rsqrt(mean_square + 1e-05) * norm_gain
    return (scaled * jax.nn.sigmoid(gate_logits.astype(jnp.float32))).astype(jnp.bfloat16)

def reference(queries, key_vectors, values, gate_logits, decay_rates, norm_gain, pool_states, pool_entry):
    head_count = decay_rates.shape[0]
    length = queries.shape[1]
    head_size = pool_states.shape[2]
    highest = lax.Precision.HIGHEST

    def one_request(items):
        query_rows, key_rows, value_rows, gate_rows, entry_id = items
        resumed = lax.dynamic_index_in_dim(pool_states, entry_id.astype(jnp.int32), 0, keepdims=False)
        resumed = resumed.astype(jnp.float32).reshape(head_count, head_size, head_size)
        query_heads = query_rows.astype(jnp.float32).reshape(length, head_count, head_size)
        key_heads = key_rows.astype(jnp.float32).reshape(length, head_count, head_size)
        value_heads = value_rows.astype(jnp.float32).reshape(length, head_count, head_size)
        positions = jnp.arange(1, length + 1).astype(jnp.float32)
        decay_now = jnp.exp(-positions[:, None] * decay_rates[None, :])
        from_state = jnp.einsum('thd,hde->the', query_heads, resumed, precision=highest) * decay_now[:, :, None]
        distance = positions[:, None] - positions[None, :]
        decay_pair = jnp.where((distance >= 0.0)[:, :, None], jnp.exp(-jnp.maximum(distance, 0.0)[:, :, None] * decay_rates), 0.0)
        scores = jnp.einsum('thd,shd->tsh', query_heads, key_heads, precision=highest) * decay_pair
        in_block = jnp.einsum('tsh,she->the', scores, value_heads, precision=highest)
        attended = (from_state + in_block).reshape(length, head_count * head_size)
        tail_decay = jnp.exp(-(float(length) - positions)[:, None] * decay_rates[None, :])
        weighted_keys = key_heads * tail_decay[:, :, None]
        updated = jnp.exp(-float(length) * decay_rates)[:, None, None] * resumed
        updated = updated + jnp.einsum('shd,she->hde', weighted_keys, value_heads, precision=highest)
        mixed_rows = finish_output(attended, gate_rows, norm_gain)
        return (mixed_rows, updated.reshape(head_count * head_size, head_size).astype(jnp.bfloat16))
    mixed, new_states = lax.map(one_request, (queries, key_vectors, values, gate_logits, pool_entry))
    return (mixed, new_states)
```

```python
import functools
import math

import jax
import jax.numpy as jnp
from jax import lax
from jax.experimental import pallas as pl
from jax.experimental.pallas import tpu as pltpu
from jax.sharding import PartitionSpec as P


def finish_output(attended, gate_logits, norm_gain):
    mean_square = jnp.mean(attended * attended, axis=-1, keepdims=True)
    scaled = attended * lax.rsqrt(mean_square + 1e-05) * norm_gain
    return (scaled * jax.nn.sigmoid(gate_logits.astype(jnp.float32))).astype(jnp.bfloat16)


def attend(query_part, key_part, value_part, resumed, rates_here):
    length = query_part.shape[1]
    highest = lax.Precision.HIGHEST
    positions = jnp.arange(1, length + 1).astype(jnp.float32)
    decay_now = jnp.exp(-positions[:, None] * rates_here[None, :])
    from_state = jnp.einsum(
        "rtgd,rgde->rtge", query_part, resumed, preferred_element_type=jnp.float32
    )
    from_state = from_state * decay_now[None, :, :, None]
    key_wide = key_part.astype(jnp.float32)
    value_wide = value_part.astype(jnp.float32)
    distance = positions[:, None] - positions[None, :]
    decay_pair = jnp.where(
        (distance >= 0.0)[:, :, None],
        jnp.exp(-jnp.maximum(distance, 0.0)[:, :, None] * rates_here),
        0.0,
    )
    scores = (
        jnp.einsum("rtgd,rsgd->rtsg", query_part, key_part, preferred_element_type=jnp.float32)
        * decay_pair[None]
    )
    in_block = jnp.einsum("rtsg,rsge->rtge", scores, value_wide, precision=highest)
    tail_decay = jnp.exp(-(float(length) - positions)[:, None] * rates_here[None, :])
    weighted_keys = key_wide * tail_decay[None, :, :, None]
    updated = jnp.exp(-float(length) * rates_here)[None, :, None, None] * resumed.astype(
        jnp.float32
    )
    updated = updated + jnp.einsum("rsgd,rsge->rgde", weighted_keys, value_wide, precision=highest)
    return (from_state + in_block, updated)


MESH = pl.DeviceIdType.MESH
TILE = 16
LANES = 128


def round_up(count, unit):
    return -(-count // unit) * unit


def plan_rows(rows):
    padded = round_up(rows, TILE)
    lead = padded - rows
    moved = round_up(padded + rows + rows - lead, TILE)
    return padded, lead, moved


def heads_kernel(
    dims,
    entry_ref,
    rates_ref,
    gain_ref,
    query_ref,
    key_ref,
    value_ref,
    gate_ref,
    pool_ref,
    mixed_ref,
    new_ref,
    entry_mine,
    entry_all,
    entry_smem,
    packed,
    block_all,
    pool_all,
    pool_now,
    att_out,
    att_in,
    gated,
    decay_now,
    decay_pair,
    decay_tail,
    entry_sems,
    pool_sems,
    block_sems,
    att_sems,
    local_sems,
):
    n, reqs, length, heads, head, stride = dims
    rows = reqs * length
    padded, lead, moved = plan_rows(rows)
    part = heads * head
    width = n * part
    shift = TILE - lead
    f32, bf16 = jnp.float32, jnp.bfloat16
    me = lax.axis_index("batch")

    def target(i):
        return lax.rem(me + lax.rem(i * stride, n), n)

    def source(i):
        return lax.rem(me + n - lax.rem(i * stride, n), n)

    barrier = pltpu.get_barrier_semaphore()

    def greet(i, carry):
        pl.semaphore_signal(barrier, inc=1, device_id={"batch": target(i)}, device_id_type=MESH)
        return carry

    lax.fori_loop(1, n, greet, 0)

    lane = lax.broadcasted_iota(jnp.int32, (8, LANES), 1)
    mine = jnp.zeros((8, LANES), jnp.int32)
    for r in range(reqs):
        mine = jnp.where(lane == r, entry_ref[r], mine)
    entry_mine[...] = mine
    entry_all[me] = mine

    def remote(src, dst, send_sem, recv_sem, peer):
        return pltpu.make_async_remote_copy(
            src_ref=src,
            dst_ref=dst,
            send_sem=send_sem,
            recv_sem=recv_sem,
            device_id={"batch": peer},
            device_id_type=MESH,
        )

    def pool_rows(h, peer):
        return pool_ref.at[0, pl.ds(pl.multiple_of(peer * part + h * head, head), head), :]

    def entry_copy(peer, slot):
        return remote(
            entry_mine, entry_all.at[slot], entry_sems.at[0, peer], entry_sems.at[1, slot], peer
        )

    def pool_copy(h, peer, slot):
        return remote(
            pool_rows(h, peer),
            pool_all.at[h, slot],
            pool_sems.at[h, 0, peer],
            pool_sems.at[h, 1, slot],
            peer,
        )

    def block_copy(h, peer, slot):
        return remote(
            packed.at[h, peer],
            block_all.at[h, slot],
            block_sems.at[h, 0, peer],
            block_sems.at[h, 1, slot],
            peer,
        )

    def att_copy(h, peer, slot):
        return remote(
            att_out.at[h, peer],
            att_in.at[h, slot],
            att_sems.at[h, 0, peer],
            att_sems.at[h, 1, slot],
            peer,
        )

    def own_pool(h):
        return pltpu.make_async_copy(pool_rows(h, me), pool_all.at[h, me], local_sems.at[0, h])

    def own_att(h):
        return pltpu.make_async_copy(att_out.at[h, me], att_in.at[h, me], local_sems.at[1, h])

    def block_of(h, peer):
        cols = pl.ds(pl.multiple_of(peer * part + h * head, head), head)
        key = key_ref[0:rows, cols].astype(f32)
        query = query_ref[0:rows, cols].astype(f32)
        value = value_ref[0:rows, cols].astype(f32)
        gap = jnp.zeros((moved - 3 * rows, head), f32)
        return jnp.concatenate([key, query[:lead], value, query[lead:], gap], axis=0).astype(bf16)

    def send_pool(h):
        def body(i, carry):
            pool_copy(h, target(i), me).start()
            return carry

        lax.fori_loop(1, n, body, 0)
        own_pool(h).start()

    def send_block(h):
        def body(i, carry):
            peer = target(i)
            packed[h, peer] = block_of(h, peer)
            block_copy(h, peer, me).start()
            return carry

        lax.fori_loop(1, n, body, 0)
        block_all[h, me] = block_of(h, me)

    def send_entries(i, carry):
        entry_copy(target(i), me).start()
        return carry

    pl.semaphore_wait(barrier, n - 1)
    lax.fori_loop(1, n, send_entries, 0)
    ahead = min(2, heads)
    for h in range(ahead):
        send_pool(h)
        send_block(h)

    def time_of(index):
        return (index // reqs + 1).astype(f32)

    def query_index(shape):
        row = lax.broadcasted_iota(jnp.int32, shape, 0)
        return jnp.maximum(jnp.where(row < TILE, row - shift, row - 2 * shift), 0)

    row_q = query_index((padded, head))
    row_k = lax.broadcasted_iota(jnp.int32, (padded, head), 0)
    pair_q = query_index((padded, LANES))
    pair_k = lax.broadcasted_iota(jnp.int32, (padded, LANES), 1)
    distance = time_of(pair_q) - time_of(pair_k)
    keep = (distance >= 0.0) & (pair_q % reqs == pair_k % reqs) & (pair_k < rows)
    for h in range(heads):
        rate = rates_ref[me * heads + h]
        decay_now[h] = jnp.exp(-time_of(row_q) * rate)
        decay_pair[h] = jnp.where(keep, jnp.exp(-jnp.maximum(distance, 0.0) * rate), 0.0)
        tail = jnp.exp(-jnp.maximum(float(length) - time_of(row_k), 0.0) * rate)
        for r in range(reqs):
            decay_tail[h, r] = jnp.where((row_k < rows) & (row_k % reqs == r), tail, 0.0)

    def prepare_gate(j, carry):
        at = pl.ds(pl.multiple_of(j * part, part), part)
        gated[:, at] = gain_ref[:, at] * jax.nn.sigmoid(gate_ref[0:rows, at].astype(f32))
        return carry

    lax.fori_loop(0, n, prepare_gate, 0)

    def wait_entries(i, carry):
        peer = source(i)
        entry_copy(peer, peer).wait_recv()
        return carry

    lax.fori_loop(1, n, wait_entries, 0)
    listing = pltpu.make_async_copy(entry_all, entry_smem, local_sems.at[2, 0])
    listing.start()
    listing.wait()

    def split(wide):
        high = wide.astype(bf16)
        return high, (wide - high.astype(f32)).astype(bf16)

    def dot(a, b, dims):
        return lax.dot_general(a, b, (dims, ((), ())), preferred_element_type=f32)

    def work(h, peer):
        starts = [pool_now[entry_smem[peer, 0, r]] for r in range(reqs)]
        key = block_all[h, peer, 0:padded]
        value = block_all[h, peer, padded : 2 * padded]
        query = jnp.concatenate(
            [block_all[h, peer, padded - TILE : padded], block_all[h, peer, 2 * padded - TILE : moved]],
            axis=0,
        )
        from_each = dot(query, jnp.concatenate(starts, axis=1), ((1,), (0,)))
        from_state = from_each[:, 0:head]
        for r in range(1, reqs):
            from_state = jnp.where(
                row_q % reqs == r, from_each[:, r * head : (r + 1) * head], from_state
            )
        scores = dot(query, block_all[h, peer, 0:LANES], ((1,), (1,))) * decay_pair[h]
        value_long = block_all[h, peer, padded : padded + LANES]
        attended = from_state * decay_now[h] + dot(
            jnp.concatenate(split(scores), axis=1),
            jnp.concatenate([value_long, value_long], axis=0),
            ((1,), (0,)),
        )
        att_out[h, peer, 0:rows] = jnp.concatenate(
            [attended[shift:TILE], attended[TILE + shift : 2 * shift + rows]], axis=0
        )
        value_wide = value.astype(f32)
        weighted = jnp.concatenate([value_wide * decay_tail[h, r] for r in range(reqs)], axis=1)
        added = dot(
            jnp.concatenate([key, key], axis=0),
            jnp.concatenate(split(weighted), axis=0),
            ((0,), (0,)),
        )
        fade = jnp.exp(jnp.full((8, head), -float(length), f32) * rates_ref[me * heads + h])[0:1]
        for r in range(reqs):
            new_ref[peer * reqs + r, pl.ds(pl.multiple_of(h * head, head), head), :] = (
                fade * starts[r].astype(f32) + added[:, r * head : (r + 1) * head]
            ).astype(bf16)

    unroll = math.gcd(n, 4)

    def each_head(h, carry):
        def take_pool(i, inner):
            peer = source(i)
            pool_copy(h, peer, peer).wait_recv()
            pool_now[peer] = pool_all[h, peer]
            return inner

        own_pool(h).wait()
        pool_now[me] = pool_all[h, me]
        lax.fori_loop(1, n, take_pool, 0)

        @pl.when(h + ahead < heads)
        def _():
            send_pool(h + ahead)
            send_block(h + ahead)

        def each_group(g, inner):
            for u in range(unroll):
                i = g * unroll + u
                peer = source(i)

                @pl.when(i > 0)
                def _():
                    block_copy(h, peer, peer).wait_recv()

            for u in range(unroll):
                work(h, source(g * unroll + u))
            for u in range(unroll):
                i = g * unroll + u
                peer = source(i)

                @pl.when(i > 0)
                def _():
                    att_copy(h, peer, me).start()

                @pl.when(i == 0)
                def _():
                    own_att(h).start()

            return inner

        lax.fori_loop(0, n // unroll, each_group, 0)
        return carry

    lax.fori_loop(0, heads, each_head, 0)

    def gather_head(h, total):
        own_att(h).wait()
        own = att_in[h, me, 0:rows]

        def gather(i, inner):
            peer = target(i)
            att_copy(h, peer, peer).wait_recv()
            here = att_in[h, peer, 0:rows]
            return inner + here * here

        return lax.fori_loop(1, n, gather, total + own * own)

    squares = lax.fori_loop(0, heads, gather_head, jnp.zeros((rows, head), f32))
    squares = jnp.sum(squares, axis=1, keepdims=True)
    scale = lax.rsqrt(squares * (1.0 / width) + 1e-05)

    def finish(j, carry):
        for h in range(heads):
            at = pl.ds(pl.multiple_of(j * part + h * head, head), head)
            mixed_ref[:, at] = (att_in[h, j, 0:rows] * scale * gated[:, at]).astype(bf16)
        return carry

    lax.fori_loop(0, n, finish, 0)

    def settle(i, carry):
        peer = target(i)
        entry_copy(peer, me).wait_send()
        for h in range(heads):
            pool_copy(h, peer, me).wait_send()
            block_copy(h, peer, me).wait_send()
            att_copy(h, peer, me).wait_send()
        return carry

    lax.fori_loop(1, n, settle, 0)


def by_heads(
    n, queries, key_vectors, values, gate_logits, decay_rates, norm_gain, pool_states, pool_entry
):
    reqs, length, width = queries.shape
    head = pool_states.shape[2]
    part = width // n
    heads = part // head
    rows = reqs * length
    padded, lead, moved = plan_rows(rows)
    sent = round_up(rows, 8)
    stride = next(s for s in range(max(n // 2 - 1, 1), 0, -1) if math.gcd(s, n) == 1)
    flat = [
        item.transpose(1, 0, 2).reshape(rows, width)
        for item in (queries, key_vectors, values, gate_logits)
    ]
    f32, bf16 = jnp.float32, jnp.bfloat16
    vmem = pl.BlockSpec(memory_space=pltpu.VMEM)
    smem = pl.BlockSpec(memory_space=pltpu.SMEM)
    anywhere = pl.BlockSpec(memory_space=pl.ANY)
    mixed, new_states = pl.pallas_call(
        functools.partial(heads_kernel, (n, reqs, length, heads, head, stride)),
        out_shape=(
            jax.ShapeDtypeStruct((rows, width), bf16),
            jax.ShapeDtypeStruct((n * reqs, part, head), bf16),
        ),
        in_specs=[smem, smem, vmem, vmem, vmem, vmem, vmem, anywhere],
        out_specs=(vmem, vmem),
        scratch_shapes=[
            pltpu.VMEM((8, LANES), jnp.int32),
            pltpu.VMEM((n, 8, LANES), jnp.int32),
            pltpu.SMEM((n, 8, LANES), jnp.int32),
            pltpu.VMEM((heads, n, moved, head), bf16),
            pltpu.VMEM((heads, n, moved, head), bf16),
            pltpu.VMEM((heads, n, head, head), bf16),
            pltpu.VMEM((n, head, head), bf16),
            pltpu.VMEM((heads, n, sent, head), f32),
            pltpu.VMEM((heads, n, sent, head), f32),
            pltpu.VMEM((rows, width), f32),
            pltpu.VMEM((heads, padded, head), f32),
            pltpu.VMEM((heads, padded, LANES), f32),
            pltpu.VMEM((heads, reqs, padded, head), f32),
            pltpu.SemaphoreType.DMA((2, n)),
            pltpu.SemaphoreType.DMA((heads, 2, n)),
            pltpu.SemaphoreType.DMA((heads, 2, n)),
            pltpu.SemaphoreType.DMA((heads, 2, n)),
            pltpu.SemaphoreType.DMA((3, heads)),
        ],
        compiler_params=pltpu.CompilerParams(
            collective_id=0, has_side_effects=True, vmem_limit_bytes=44 * 1024 * 1024
        ),
    )(pool_entry, decay_rates, norm_gain.reshape(1, width), *flat, pool_states)
    return mixed.reshape(length, reqs, width).transpose(1, 0, 2), new_states


def on_device(
    queries, key_vectors, values, gate_logits, decay_rates, norm_gain, pool_states, pool_entry
):
    req_dev, length, feature_width = queries.shape
    head_count = decay_rates.shape[0]
    head_size = pool_states.shape[2]
    ranks = lax.axis_size("batch")
    rows = req_dev * length
    lead = -rows % TILE
    if (
        ranks > 1
        and feature_width % (ranks * head_size) == 0
        and pool_states.shape[0] == 1
        and head_size % LANES == 0
        and 0 < lead < min(rows, TILE)
        and rows <= LANES
        and plan_rows(rows)[0] + LANES <= plan_rows(rows)[2]
        and plan_rows(rows)[2] == 3 * plan_rows(rows)[0] - 2 * TILE
    ):
        return by_heads(
            ranks, queries, key_vectors, values, gate_logits, decay_rates, norm_gain, pool_states, pool_entry
        )
    entries = lax.all_gather(pool_entry, "batch", axis=0, tiled=True)
    spread = lax.all_to_all(pool_states, "batch", split_axis=1, concat_axis=0, tiled=True)
    chosen = jnp.take(spread, entries, axis=0)
    resumed = lax.all_to_all(chosen, "batch", split_axis=0, concat_axis=1, tiled=True)
    resumed = resumed.reshape(req_dev, head_count, head_size, head_size)
    shaped = (req_dev, length, head_count, head_size)
    attended, updated = attend(
        queries.reshape(shaped),
        key_vectors.reshape(shaped),
        values.reshape(shaped),
        resumed,
        decay_rates,
    )
    attended = attended.reshape(req_dev, length, feature_width)
    local_states = updated.astype(jnp.bfloat16).reshape(req_dev, feature_width, head_size)
    new_states = lax.all_to_all(local_states, "batch", split_axis=1, concat_axis=0, tiled=True)
    mixed = finish_output(attended, gate_logits, norm_gain)
    return (mixed, new_states)


def solution(mesh):
    placed = (
        P(("groups", "batch"), None, None),
        P(("groups", "batch"), None, None),
        P(("groups", "batch"), None, None),
        P(("groups", "batch"), None, None),
        P(),
        P(),
        P(("groups", "batch"), None, None),
        P(("groups", "batch")),
    )
    return jax.shard_map(
        on_device,
        mesh=mesh,
        in_specs=placed,
        out_specs=(P(("groups", "batch"), None, None), P("groups", "batch", None)),
        check_vma=False,
    )
```

```python
import functools
import math

import jax
import jax.numpy as jnp
from jax import lax
from jax.experimental import pallas as pl
from jax.experimental.pallas import tpu as pltpu
from jax.sharding import PartitionSpec as P


def finish_output(attended, gate_logits, norm_gain):
    mean_square = jnp.mean(attended * attended, axis=-1, keepdims=True)
    scaled = attended * lax.rsqrt(mean_square + 1e-05) * norm_gain
    return (scaled * jax.nn.sigmoid(gate_logits.astype(jnp.float32))).astype(jnp.bfloat16)


def attend(query_part, key_part, value_part, resumed, rates_here):
    length = query_part.shape[1]
    highest = lax.Precision.HIGHEST
    positions = jnp.arange(1, length + 1).astype(jnp.float32)
    decay_now = jnp.exp(-positions[:, None] * rates_here[None, :])
    from_state = jnp.einsum(
        "rtgd,rgde->rtge", query_part, resumed, preferred_element_type=jnp.float32
    )
    from_state = from_state * decay_now[None, :, :, None]
    key_wide = key_part.astype(jnp.float32)
    value_wide = value_part.astype(jnp.float32)
    distance = positions[:, None] - positions[None, :]
    decay_pair = jnp.where(
        (distance >= 0.0)[:, :, None],
        jnp.exp(-jnp.maximum(distance, 0.0)[:, :, None] * rates_here),
        0.0,
    )
    scores = (
        jnp.einsum("rtgd,rsgd->rtsg", query_part, key_part, preferred_element_type=jnp.float32)
        * decay_pair[None]
    )
    in_block = jnp.einsum("rtsg,rsge->rtge", scores, value_wide, precision=highest)
    tail_decay = jnp.exp(-(float(length) - positions)[:, None] * rates_here[None, :])
    weighted_keys = key_wide * tail_decay[None, :, :, None]
    updated = jnp.exp(-float(length) * rates_here)[None, :, None, None] * resumed.astype(
        jnp.float32
    )
    updated = updated + jnp.einsum("rsgd,rsge->rgde", weighted_keys, value_wide, precision=highest)
    return (from_state + in_block, updated)


MESH = pl.DeviceIdType.MESH
TILE = 16
LANES = 128


def round_up(count, unit):
    return -(-count // unit) * unit


def plan_rows(rows):
    padded = round_up(rows, TILE)
    lead = padded - rows
    moved = round_up(padded + rows + rows - lead, TILE)
    return padded, lead, moved


def heads_kernel(
    dims,
    entry_ref,
    rates_ref,
    gain_ref,
    query_ref,
    key_ref,
    value_ref,
    gate_ref,
    pool_ref,
    mixed_ref,
    new_ref,
    entry_mine,
    entry_all,
    entry_smem,
    packed,
    block_all,
    pool_all,
    pool_now,
    att_out,
    att_in,
    gated,
    decay_now,
    decay_pair,
    decay_tail,
    entry_sems,
    pool_sems,
    block_sems,
    att_sems,
    local_sems,
):
    n, reqs, length, heads, head = dims
    rows = reqs * length
    padded, lead, moved = plan_rows(rows)
    part = heads * head
    width = n * part
    shift = TILE - lead
    f32, bf16 = jnp.float32, jnp.bfloat16
    me = lax.axis_index("batch")

    def partner(i):
        step = (i % 2) * (n // 2) + i // 2
        peer = 0
        bit = 1
        while bit < n:
            peer = peer + ((me // bit + step // bit) % 2) * bit
            bit *= 2
        return peer

    barrier = pltpu.get_barrier_semaphore()

    def greet(i, carry):
        pl.semaphore_signal(barrier, inc=1, device_id={"batch": partner(i)}, device_id_type=MESH)
        return carry

    lax.fori_loop(1, n, greet, 0)

    lane = lax.broadcasted_iota(jnp.int32, (8, LANES), 1)
    mine = jnp.zeros((8, LANES), jnp.int32)
    for r in range(reqs):
        mine = jnp.where(lane == r, entry_ref[r], mine)
    entry_mine[...] = mine
    entry_all[me] = mine

    def remote(src, dst, send_sem, recv_sem, peer):
        return pltpu.make_async_remote_copy(
            src_ref=src,
            dst_ref=dst,
            send_sem=send_sem,
            recv_sem=recv_sem,
            device_id={"batch": peer},
            device_id_type=MESH,
        )

    def pool_rows(h, peer):
        return pool_ref.at[0, pl.ds(pl.multiple_of(peer * part + h * head, head), head), :]

    def entry_copy(peer, slot):
        return remote(
            entry_mine, entry_all.at[slot], entry_sems.at[0, peer], entry_sems.at[1, slot], peer
        )

    def pool_copy(h, peer, slot):
        return remote(
            pool_rows(h, peer),
            pool_all.at[h, slot],
            pool_sems.at[h, 0, peer],
            pool_sems.at[h, 1, slot],
            peer,
        )

    def block_copy(h, peer, slot):
        return remote(
            packed.at[h, peer],
            block_all.at[h, slot],
            block_sems.at[h, 0, peer],
            block_sems.at[h, 1, slot],
            peer,
        )

    def att_copy(h, peer, slot):
        return remote(
            att_out.at[h, peer],
            att_in.at[h, slot],
            att_sems.at[h, 0, peer],
            att_sems.at[h, 1, slot],
            peer,
        )

    def own_pool(h):
        return pltpu.make_async_copy(pool_rows(h, me), pool_all.at[h, me], local_sems.at[0, h])

    def own_att(h):
        return pltpu.make_async_copy(att_out.at[h, me], att_in.at[h, me], local_sems.at[1, h])

    def block_of(h, peer):
        cols = pl.ds(pl.multiple_of(peer * part + h * head, head), head)
        key = key_ref[0:rows, cols].astype(f32)
        query = query_ref[0:rows, cols].astype(f32)
        value = value_ref[0:rows, cols].astype(f32)
        gap = jnp.zeros((moved - 3 * rows, head), f32)
        return jnp.concatenate([key, query[:lead], value, query[lead:], gap], axis=0).astype(bf16)

    def send_pool(h):
        def body(i, carry):
            pool_copy(h, partner(i), me).start()
            return carry

        lax.fori_loop(1, n, body, 0)
        own_pool(h).start()

    def send_block(h):
        def body(i, carry):
            peer = partner(i)
            packed[h, peer] = block_of(h, peer)
            block_copy(h, peer, me).start()
            return carry

        lax.fori_loop(1, n, body, 0)
        block_all[h, me] = block_of(h, me)

    def send_entries(i, carry):
        entry_copy(partner(i), me).start()
        return carry

    pl.semaphore_wait(barrier, n - 1)
    lax.fori_loop(1, n, send_entries, 0)
    ahead = min(2, heads)
    for h in range(ahead):
        send_pool(h)
        send_block(h)

    def time_of(index):
        return (index // reqs + 1).astype(f32)

    def query_index(shape):
        row = lax.broadcasted_iota(jnp.int32, shape, 0)
        return jnp.maximum(jnp.where(row < TILE, row - shift, row - 2 * shift), 0)

    row_q = query_index((padded, head))
    row_k = lax.broadcasted_iota(jnp.int32, (padded, head), 0)
    pair_q = query_index((padded, LANES))
    pair_k = lax.broadcasted_iota(jnp.int32, (padded, LANES), 1)
    distance = time_of(pair_q) - time_of(pair_k)
    keep = (distance >= 0.0) & (pair_q % reqs == pair_k % reqs) & (pair_k < rows)
    for h in range(heads):
        rate = rates_ref[me * heads + h]
        decay_now[h] = jnp.exp(-time_of(row_q) * rate)
        decay_pair[h] = jnp.where(keep, jnp.exp(-jnp.maximum(distance, 0.0) * rate), 0.0)
        tail = jnp.exp(-jnp.maximum(float(length) - time_of(row_k), 0.0) * rate)
        for r in range(reqs):
            decay_tail[h, r] = jnp.where((row_k < rows) & (row_k % reqs == r), tail, 0.0)

    def prepare_gate(j, carry):
        at = pl.ds(pl.multiple_of(j * part, part), part)
        gated[:, at] = gain_ref[:, at] * jax.nn.sigmoid(gate_ref[0:rows, at].astype(f32))
        return carry

    lax.fori_loop(0, n, prepare_gate, 0)

    def wait_entries(i, carry):
        peer = partner(i)
        entry_copy(peer, peer).wait_recv()
        return carry

    lax.fori_loop(1, n, wait_entries, 0)
    listing = pltpu.make_async_copy(entry_all, entry_smem, local_sems.at[2, 0])
    listing.start()
    listing.wait()

    def split(wide):
        high = wide.astype(bf16)
        return high, (wide - high.astype(f32)).astype(bf16)

    def dot(a, b, dims):
        return lax.dot_general(a, b, (dims, ((), ())), preferred_element_type=f32)

    def work(h, peer):
        starts = [pool_now[entry_smem[peer, 0, r]] for r in range(reqs)]
        key = block_all[h, peer, 0:padded]
        value = block_all[h, peer, padded : 2 * padded]
        query = jnp.concatenate(
            [block_all[h, peer, padded - TILE : padded], block_all[h, peer, 2 * padded - TILE : moved]],
            axis=0,
        )
        from_each = dot(query, jnp.concatenate(starts, axis=1), ((1,), (0,)))
        from_state = from_each[:, 0:head]
        for r in range(1, reqs):
            from_state = jnp.where(
                row_q % reqs == r, from_each[:, r * head : (r + 1) * head], from_state
            )
        scores = dot(query, block_all[h, peer, 0:LANES], ((1,), (1,))) * decay_pair[h]
        value_long = block_all[h, peer, padded : padded + LANES]
        attended = from_state * decay_now[h] + dot(
            jnp.concatenate(split(scores), axis=1),
            jnp.concatenate([value_long, value_long], axis=0),
            ((1,), (0,)),
        )
        att_out[h, peer, 0:rows] = jnp.concatenate(
            [attended[shift:TILE], attended[TILE + shift : 2 * shift + rows]], axis=0
        )
        value_wide = value.astype(f32)
        weighted = jnp.concatenate([value_wide * decay_tail[h, r] for r in range(reqs)], axis=1)
        added = dot(
            jnp.concatenate([key, key], axis=0),
            jnp.concatenate(split(weighted), axis=0),
            ((0,), (0,)),
        )
        fade = jnp.exp(jnp.full((8, head), -float(length), f32) * rates_ref[me * heads + h])[0:1]
        for r in range(reqs):
            new_ref[peer * reqs + r, pl.ds(pl.multiple_of(h * head, head), head), :] = (
                fade * starts[r].astype(f32) + added[:, r * head : (r + 1) * head]
            ).astype(bf16)

    unroll = math.gcd(n, 4)

    def each_head(h, carry):
        def take_pool(i, inner):
            peer = partner(i)
            pool_copy(h, peer, peer).wait_recv()
            pool_now[peer] = pool_all[h, peer]
            return inner

        own_pool(h).wait()
        pool_now[me] = pool_all[h, me]
        lax.fori_loop(1, n, take_pool, 0)

        @pl.when(h + ahead < heads)
        def _():
            send_pool(h + ahead)
            send_block(h + ahead)

        def each_group(g, inner):
            for u in range(unroll):
                i = g * unroll + u
                peer = partner(i)

                @pl.when(i > 0)
                def _():
                    block_copy(h, peer, peer).wait_recv()

            for u in range(unroll):
                work(h, partner(g * unroll + u))
            for u in range(unroll):
                i = g * unroll + u
                peer = partner(i)

                @pl.when(i > 0)
                def _():
                    att_copy(h, peer, me).start()

                @pl.when(i == 0)
                def _():
                    own_att(h).start()

            return inner

        lax.fori_loop(0, n // unroll, each_group, 0)
        return carry

    lax.fori_loop(0, heads, each_head, 0)

    def gather_head(h, total):
        own_att(h).wait()
        own = att_in[h, me, 0:rows]

        def gather(i, inner):
            peer = partner(i)
            att_copy(h, peer, peer).wait_recv()
            here = att_in[h, peer, 0:rows]
            return inner + here * here

        return lax.fori_loop(1, n, gather, total + own * own)

    squares = lax.fori_loop(0, heads, gather_head, jnp.zeros((rows, head), f32))
    squares = jnp.sum(squares, axis=1, keepdims=True)
    scale = lax.rsqrt(squares * (1.0 / width) + 1e-05)

    def finish(j, carry):
        for h in range(heads):
            at = pl.ds(pl.multiple_of(j * part + h * head, head), head)
            mixed_ref[:, at] = (att_in[h, j, 0:rows] * scale * gated[:, at]).astype(bf16)
        return carry

    lax.fori_loop(0, n, finish, 0)

    def settle(i, carry):
        peer = partner(i)
        entry_copy(peer, me).wait_send()
        for h in range(heads):
            pool_copy(h, peer, me).wait_send()
            block_copy(h, peer, me).wait_send()
            att_copy(h, peer, me).wait_send()
        return carry

    lax.fori_loop(1, n, settle, 0)


def by_heads(
    n, queries, key_vectors, values, gate_logits, decay_rates, norm_gain, pool_states, pool_entry
):
    reqs, length, width = queries.shape
    head = pool_states.shape[2]
    part = width // n
    heads = part // head
    rows = reqs * length
    padded, lead, moved = plan_rows(rows)
    sent = round_up(rows, 8)
    flat = [
        item.transpose(1, 0, 2).reshape(rows, width)
        for item in (queries, key_vectors, values, gate_logits)
    ]
    f32, bf16 = jnp.float32, jnp.bfloat16
    vmem = pl.BlockSpec(memory_space=pltpu.VMEM)
    smem = pl.BlockSpec(memory_space=pltpu.SMEM)
    anywhere = pl.BlockSpec(memory_space=pl.ANY)
    mixed, new_states = pl.pallas_call(
        functools.partial(heads_kernel, (n, reqs, length, heads, head)),
        out_shape=(
            jax.ShapeDtypeStruct((rows, width), bf16),
            jax.ShapeDtypeStruct((n * reqs, part, head), bf16),
        ),
        in_specs=[smem, smem, vmem, vmem, vmem, vmem, vmem, anywhere],
        out_specs=(vmem, vmem),
        scratch_shapes=[
            pltpu.VMEM((8, LANES), jnp.int32),
            pltpu.VMEM((n, 8, LANES), jnp.int32),
            pltpu.SMEM((n, 8, LANES), jnp.int32),
            pltpu.VMEM((heads, n, moved, head), bf16),
            pltpu.VMEM((heads, n, moved, head), bf16),
            pltpu.VMEM((heads, n, head, head), bf16),
            pltpu.VMEM((n, head, head), bf16),
            pltpu.VMEM((heads, n, sent, head), f32),
            pltpu.VMEM((heads, n, sent, head), f32),
            pltpu.VMEM((rows, width), f32),
            pltpu.VMEM((heads, padded, head), f32),
            pltpu.VMEM((heads, padded, LANES), f32),
            pltpu.VMEM((heads, reqs, padded, head), f32),
            pltpu.SemaphoreType.DMA((2, n)),
            pltpu.SemaphoreType.DMA((heads, 2, n)),
            pltpu.SemaphoreType.DMA((heads, 2, n)),
            pltpu.SemaphoreType.DMA((heads, 2, n)),
            pltpu.SemaphoreType.DMA((3, heads)),
        ],
        compiler_params=pltpu.CompilerParams(
            collective_id=0, has_side_effects=True, vmem_limit_bytes=44 * 1024 * 1024
        ),
    )(pool_entry, decay_rates, norm_gain.reshape(1, width), *flat, pool_states)
    return mixed.reshape(length, reqs, width).transpose(1, 0, 2), new_states


def on_device(
    queries, key_vectors, values, gate_logits, decay_rates, norm_gain, pool_states, pool_entry
):
    req_dev, length, feature_width = queries.shape
    head_count = decay_rates.shape[0]
    head_size = pool_states.shape[2]
    ranks = lax.axis_size("batch")
    rows = req_dev * length
    lead = -rows % TILE
    if (
        ranks > 1
        and ranks & (ranks - 1) == 0
        and feature_width % (ranks * head_size) == 0
        and pool_states.shape[0] == 1
        and head_size % LANES == 0
        and 0 < lead < min(rows, TILE)
        and rows <= LANES
        and plan_rows(rows)[0] + LANES <= plan_rows(rows)[2]
        and plan_rows(rows)[2] == 3 * plan_rows(rows)[0] - 2 * TILE
    ):
        return by_heads(
            ranks, queries, key_vectors, values, gate_logits, decay_rates, norm_gain, pool_states, pool_entry
        )
    entries = lax.all_gather(pool_entry, "batch", axis=0, tiled=True)
    spread = lax.all_to_all(pool_states, "batch", split_axis=1, concat_axis=0, tiled=True)
    chosen = jnp.take(spread, entries, axis=0)
    resumed = lax.all_to_all(chosen, "batch", split_axis=0, concat_axis=1, tiled=True)
    resumed = resumed.reshape(req_dev, head_count, head_size, head_size)
    shaped = (req_dev, length, head_count, head_size)
    attended, updated = attend(
        queries.reshape(shaped),
        key_vectors.reshape(shaped),
        values.reshape(shaped),
        resumed,
        decay_rates,
    )
    attended = attended.reshape(req_dev, length, feature_width)
    local_states = updated.astype(jnp.bfloat16).reshape(req_dev, feature_width, head_size)
    new_states = lax.all_to_all(local_states, "batch", split_axis=1, concat_axis=0, tiled=True)
    mixed = finish_output(attended, gate_logits, norm_gain)
    return (mixed, new_states)


def solution(mesh):
    placed = (
        P(("groups", "batch"), None, None),
        P(("groups", "batch"), None, None),
        P(("groups", "batch"), None, None),
        P(("groups", "batch"), None, None),
        P(),
        P(),
        P(("groups", "batch"), None, None),
        P(("groups", "batch")),
    )
    return jax.shard_map(
        on_device,
        mesh=mesh,
        in_specs=placed,
        out_specs=(P(("groups", "batch"), None, None), P("groups", "batch", None)),
        check_vma=False,
    )
```

```python
import functools
import math

import jax
import jax.numpy as jnp
from jax import lax
from jax.experimental import pallas as pl
from jax.experimental.pallas import tpu as pltpu
from jax.sharding import PartitionSpec as P


def finish_output(attended, gate_logits, norm_gain):
    mean_square = jnp.mean(attended * attended, axis=-1, keepdims=True)
    scaled = attended * lax.rsqrt(mean_square + 1e-05) * norm_gain
    return (scaled * jax.nn.sigmoid(gate_logits.astype(jnp.float32))).astype(jnp.bfloat16)


def attend(query_part, key_part, value_part, resumed, rates_here):
    length = query_part.shape[1]
    highest = lax.Precision.HIGHEST
    positions = jnp.arange(1, length + 1).astype(jnp.float32)
    decay_now = jnp.exp(-positions[:, None] * rates_here[None, :])
    from_state = jnp.einsum(
        "rtgd,rgde->rtge", query_part, resumed, preferred_element_type=jnp.float32
    )
    from_state = from_state * decay_now[None, :, :, None]
    key_wide = key_part.astype(jnp.float32)
    value_wide = value_part.astype(jnp.float32)
    distance = positions[:, None] - positions[None, :]
    decay_pair = jnp.where(
        (distance >= 0.0)[:, :, None],
        jnp.exp(-jnp.maximum(distance, 0.0)[:, :, None] * rates_here),
        0.0,
    )
    scores = (
        jnp.einsum("rtgd,rsgd->rtsg", query_part, key_part, preferred_element_type=jnp.float32)
        * decay_pair[None]
    )
    in_block = jnp.einsum("rtsg,rsge->rtge", scores, value_wide, precision=highest)
    tail_decay = jnp.exp(-(float(length) - positions)[:, None] * rates_here[None, :])
    weighted_keys = key_wide * tail_decay[None, :, :, None]
    updated = jnp.exp(-float(length) * rates_here)[None, :, None, None] * resumed.astype(
        jnp.float32
    )
    updated = updated + jnp.einsum("rsgd,rsge->rgde", weighted_keys, value_wide, precision=highest)
    return (from_state + in_block, updated)


MESH = pl.DeviceIdType.MESH
TILE = 16
LANES = 128
CODE_TOP = 32000.0


def round_up(count, unit):
    return -(-count // unit) * unit


def plan_rows(rows):
    padded = round_up(rows, TILE)
    lead = padded - rows
    moved = round_up(padded + rows + rows - lead, TILE)
    return padded, lead, moved


def heads_kernel(
    dims,
    entry_ref,
    rates_ref,
    gain_ref,
    query_ref,
    key_ref,
    value_ref,
    gate_ref,
    pool_ref,
    mixed_ref,
    new_ref,
    entry_mine,
    entry_all,
    entry_smem,
    packed,
    block_all,
    pool_all,
    pool_now,
    att_out,
    att_in,
    att_wide,
    gated,
    decay_now,
    decay_pair,
    decay_tail,
    entry_sems,
    pool_sems,
    block_sems,
    att_sems,
    local_sems,
):
    n, reqs, length, heads, head = dims
    rows = reqs * length
    padded, lead, moved = plan_rows(rows)
    part = heads * head
    width = n * part
    shift = TILE - lead
    f32, bf16 = jnp.float32, jnp.bfloat16
    me = lax.axis_index("batch")

    def partner(i):
        step = (i % 2) * (n // 2) + i // 2
        peer = 0
        bit = 1
        while bit < n:
            peer = peer + ((me // bit + step // bit) % 2) * bit
            bit *= 2
        return peer

    barrier = pltpu.get_barrier_semaphore()

    def greet(i, carry):
        pl.semaphore_signal(barrier, inc=1, device_id={"batch": partner(i)}, device_id_type=MESH)
        return carry

    lax.fori_loop(1, n, greet, 0)

    lane = lax.broadcasted_iota(jnp.int32, (8, LANES), 1)
    mine = jnp.zeros((8, LANES), jnp.int32)
    for r in range(reqs):
        mine = jnp.where(lane == r, entry_ref[r], mine)
    entry_mine[...] = mine
    entry_all[me] = mine

    def remote(src, dst, send_sem, recv_sem, peer):
        return pltpu.make_async_remote_copy(
            src_ref=src,
            dst_ref=dst,
            send_sem=send_sem,
            recv_sem=recv_sem,
            device_id={"batch": peer},
            device_id_type=MESH,
        )

    def pool_rows(h, peer):
        return pool_ref.at[0, pl.ds(pl.multiple_of(peer * part + h * head, head), head), :]

    def entry_copy(peer, slot):
        return remote(
            entry_mine, entry_all.at[slot], entry_sems.at[0, peer], entry_sems.at[1, slot], peer
        )

    def pool_copy(h, peer, slot):
        return remote(
            pool_rows(h, peer),
            pool_all.at[h, slot],
            pool_sems.at[h, 0, peer],
            pool_sems.at[h, 1, slot],
            peer,
        )

    def block_copy(h, peer, slot):
        return remote(
            packed.at[h, peer],
            block_all.at[h, slot],
            block_sems.at[h, 0, peer],
            block_sems.at[h, 1, slot],
            peer,
        )

    def att_copy(h, peer, slot):
        return remote(
            att_out.at[h, peer],
            att_in.at[h, slot],
            att_sems.at[h, 0, peer],
            att_sems.at[h, 1, slot],
            peer,
        )

    def own_pool(h):
        return pltpu.make_async_copy(pool_rows(h, me), pool_all.at[h, me], local_sems.at[0, h])

    def own_att(h):
        return pltpu.make_async_copy(att_out.at[h, me], att_in.at[h, me], local_sems.at[1, h])

    def block_of(h, peer):
        cols = pl.ds(pl.multiple_of(peer * part + h * head, head), head)
        key = key_ref[0:rows, cols].astype(f32)
        query = query_ref[0:rows, cols].astype(f32)
        value = value_ref[0:rows, cols].astype(f32)
        gap = jnp.zeros((moved - 3 * rows, head), f32)
        return jnp.concatenate([key, query[:lead], value, query[lead:], gap], axis=0).astype(bf16)

    def send_pool(h):
        def body(i, carry):
            pool_copy(h, partner(i), me).start()
            return carry

        lax.fori_loop(1, n, body, 0)
        own_pool(h).start()

    def send_block(h):
        def body(i, carry):
            peer = partner(i)
            packed[h, peer] = block_of(h, peer)
            block_copy(h, peer, me).start()
            return carry

        lax.fori_loop(1, n, body, 0)
        block_all[h, me] = block_of(h, me)

    def send_entries(i, carry):
        entry_copy(partner(i), me).start()
        return carry

    pl.semaphore_wait(barrier, n - 1)
    lax.fori_loop(1, n, send_entries, 0)
    ahead = min(2, heads)
    for h in range(ahead):
        send_pool(h)
        send_block(h)

    def time_of(index):
        return (index // reqs + 1).astype(f32)

    def query_index(shape):
        row = lax.broadcasted_iota(jnp.int32, shape, 0)
        return jnp.maximum(jnp.where(row < TILE, row - shift, row - 2 * shift), 0)

    row_q = query_index((padded, head))
    row_k = lax.broadcasted_iota(jnp.int32, (padded, head), 0)
    pair_q = query_index((padded, LANES))
    pair_k = lax.broadcasted_iota(jnp.int32, (padded, LANES), 1)
    distance = time_of(pair_q) - time_of(pair_k)
    keep = (distance >= 0.0) & (pair_q % reqs == pair_k % reqs) & (pair_k < rows)
    for h in range(heads):
        rate = rates_ref[me * heads + h]
        decay_now[h] = jnp.exp(-time_of(row_q) * rate)
        decay_pair[h] = jnp.where(keep, jnp.exp(-jnp.maximum(distance, 0.0) * rate), 0.0)
        tail = jnp.exp(-jnp.maximum(float(length) - time_of(row_k), 0.0) * rate)
        for r in range(reqs):
            decay_tail[h, r] = jnp.where((row_k < rows) & (row_k % reqs == r), tail, 0.0)

    def prepare_gate(j, carry):
        at = pl.ds(pl.multiple_of(j * part, part), part)
        gated[:, at] = gain_ref[:, at] * jax.nn.sigmoid(gate_ref[0:rows, at].astype(f32))
        return carry

    lax.fori_loop(0, n, prepare_gate, 0)

    def wait_entries(i, carry):
        peer = partner(i)
        entry_copy(peer, peer).wait_recv()
        return carry

    lax.fori_loop(1, n, wait_entries, 0)
    listing = pltpu.make_async_copy(entry_all, entry_smem, local_sems.at[2, 0])
    listing.start()
    listing.wait()

    def split(wide):
        high = wide.astype(bf16)
        return high, (wide - high.astype(f32)).astype(bf16)

    def dot(a, b, dims):
        return lax.dot_general(a, b, (dims, ((), ())), preferred_element_type=f32)

    code_row = lax.broadcasted_iota(jnp.int32, (padded, head), 0)
    code_col = lax.broadcasted_iota(jnp.int32, (padded, head), 1)

    def encode(wide):
        size = jnp.abs(wide)
        power = jnp.ceil(jnp.log2(jnp.maximum(jnp.max(size, axis=1, keepdims=True), 1e-30)))
        root = jnp.sqrt(size * jnp.exp2(-power)) * CODE_TOP
        code = jnp.where(wide < 0.0, -root, root)
        powers = jnp.sum(jnp.where(code_row == code_col, power, 0.0), axis=0, keepdims=True)
        code = jnp.where(code_row == rows, powers, code)
        return jnp.round(code).astype(jnp.int32).astype(jnp.int16)

    def decode(code):
        wide = code.astype(jnp.int32).astype(f32)
        powers = jnp.where(code_row == code_col, wide[rows : rows + 1], 0.0)
        power = jnp.exp2(jnp.sum(powers, axis=1, keepdims=True)) * (1.0 / (CODE_TOP * CODE_TOP))
        return (wide * jnp.abs(wide) * power)[0:rows]

    def work(h, peer):
        starts = [pool_now[entry_smem[peer, 0, r]] for r in range(reqs)]
        key = block_all[h, peer, 0:padded]
        value = block_all[h, peer, padded : 2 * padded]
        query = jnp.concatenate(
            [block_all[h, peer, padded - TILE : padded], block_all[h, peer, 2 * padded - TILE : moved]],
            axis=0,
        )
        from_each = dot(query, jnp.concatenate(starts, axis=1), ((1,), (0,)))
        from_state = from_each[:, 0:head]
        for r in range(1, reqs):
            from_state = jnp.where(
                row_q % reqs == r, from_each[:, r * head : (r + 1) * head], from_state
            )
        scores = dot(query, block_all[h, peer, 0:LANES], ((1,), (1,))) * decay_pair[h]
        value_long = block_all[h, peer, padded : padded + LANES]
        attended = from_state * decay_now[h] + dot(
            jnp.concatenate(split(scores), axis=1),
            jnp.concatenate([value_long, value_long], axis=0),
            ((1,), (0,)),
        )
        att_out[h, peer] = encode(
            jnp.concatenate(
                [
                    attended[shift:TILE],
                    attended[TILE + shift : 2 * shift + rows],
                    jnp.zeros((padded - rows, head), f32),
                ],
                axis=0,
            )
        )
        value_wide = value.astype(f32)
        weighted = jnp.concatenate([value_wide * decay_tail[h, r] for r in range(reqs)], axis=1)
        added = dot(
            jnp.concatenate([key, key], axis=0),
            jnp.concatenate(split(weighted), axis=0),
            ((0,), (0,)),
        )
        fade = jnp.exp(jnp.full((8, head), -float(length), f32) * rates_ref[me * heads + h])[0:1]
        for r in range(reqs):
            new_ref[peer * reqs + r, pl.ds(pl.multiple_of(h * head, head), head), :] = (
                fade * starts[r].astype(f32) + added[:, r * head : (r + 1) * head]
            ).astype(bf16)

    unroll = math.gcd(n, 4)

    def each_head(h, carry):
        def take_pool(i, inner):
            peer = partner(i)
            pool_copy(h, peer, peer).wait_recv()
            pool_now[peer] = pool_all[h, peer]
            return inner

        own_pool(h).wait()
        pool_now[me] = pool_all[h, me]
        lax.fori_loop(1, n, take_pool, 0)

        @pl.when(h + ahead < heads)
        def _():
            send_pool(h + ahead)
            send_block(h + ahead)

        def each_group(g, inner):
            for u in range(unroll):
                i = g * unroll + u
                peer = partner(i)

                @pl.when(i > 0)
                def _():
                    block_copy(h, peer, peer).wait_recv()

            for u in range(unroll):
                work(h, partner(g * unroll + u))
            for u in range(unroll):
                i = g * unroll + u
                peer = partner(i)

                @pl.when(i > 0)
                def _():
                    att_copy(h, peer, me).start()

                @pl.when(i == 0)
                def _():
                    own_att(h).start()

            return inner

        lax.fori_loop(0, n // unroll, each_group, 0)
        return carry

    lax.fori_loop(0, heads, each_head, 0)

    def gather_head(h, total):
        own_att(h).wait()
        own = decode(att_in[h, me])
        att_wide[h, me] = own

        def gather(i, inner):
            peer = partner(i)
            att_copy(h, peer, peer).wait_recv()
            here = decode(att_in[h, peer])
            att_wide[h, peer] = here
            return inner + here * here

        return lax.fori_loop(1, n, gather, total + own * own)

    squares = lax.fori_loop(0, heads, gather_head, jnp.zeros((rows, head), f32))
    squares = jnp.sum(squares, axis=1, keepdims=True)
    scale = lax.rsqrt(squares * (1.0 / width) + 1e-05)

    def finish(j, carry):
        for h in range(heads):
            at = pl.ds(pl.multiple_of(j * part + h * head, head), head)
            mixed_ref[:, at] = (att_wide[h, j] * scale * gated[:, at]).astype(bf16)
        return carry

    lax.fori_loop(0, n, finish, 0)

    def settle(i, carry):
        peer = partner(i)
        entry_copy(peer, me).wait_send()
        for h in range(heads):
            pool_copy(h, peer, me).wait_send()
            block_copy(h, peer, me).wait_send()
            att_copy(h, peer, me).wait_send()
        return carry

    lax.fori_loop(1, n, settle, 0)


def by_heads(
    n, queries, key_vectors, values, gate_logits, decay_rates, norm_gain, pool_states, pool_entry
):
    reqs, length, width = queries.shape
    head = pool_states.shape[2]
    part = width // n
    heads = part // head
    rows = reqs * length
    padded, lead, moved = plan_rows(rows)
    flat = [
        item.transpose(1, 0, 2).reshape(rows, width)
        for item in (queries, key_vectors, values, gate_logits)
    ]
    f32, bf16 = jnp.float32, jnp.bfloat16
    vmem = pl.BlockSpec(memory_space=pltpu.VMEM)
    smem = pl.BlockSpec(memory_space=pltpu.SMEM)
    anywhere = pl.BlockSpec(memory_space=pl.ANY)
    mixed, new_states = pl.pallas_call(
        functools.partial(heads_kernel, (n, reqs, length, heads, head)),
        out_shape=(
            jax.ShapeDtypeStruct((rows, width), bf16),
            jax.ShapeDtypeStruct((n * reqs, part, head), bf16),
        ),
        in_specs=[smem, smem, vmem, vmem, vmem, vmem, vmem, anywhere],
        out_specs=(vmem, vmem),
        scratch_shapes=[
            pltpu.VMEM((8, LANES), jnp.int32),
            pltpu.VMEM((n, 8, LANES), jnp.int32),
            pltpu.SMEM((n, 8, LANES), jnp.int32),
            pltpu.VMEM((heads, n, moved, head), bf16),
            pltpu.VMEM((heads, n, moved, head), bf16),
            pltpu.VMEM((heads, n, head, head), bf16),
            pltpu.VMEM((n, head, head), bf16),
            pltpu.VMEM((heads, n, padded, head), jnp.int16),
            pltpu.VMEM((heads, n, padded, head), jnp.int16),
            pltpu.VMEM((heads, n, rows, head), f32),
            pltpu.VMEM((rows, width), f32),
            pltpu.VMEM((heads, padded, head), f32),
            pltpu.VMEM((heads, padded, LANES), f32),
            pltpu.VMEM((heads, reqs, padded, head), f32),
            pltpu.SemaphoreType.DMA((2, n)),
            pltpu.SemaphoreType.DMA((heads, 2, n)),
            pltpu.SemaphoreType.DMA((heads, 2, n)),
            pltpu.SemaphoreType.DMA((heads, 2, n)),
            pltpu.SemaphoreType.DMA((3, heads)),
        ],
        compiler_params=pltpu.CompilerParams(
            collective_id=0, has_side_effects=True, vmem_limit_bytes=44 * 1024 * 1024
        ),
    )(pool_entry, decay_rates, norm_gain.reshape(1, width), *flat, pool_states)
    return mixed.reshape(length, reqs, width).transpose(1, 0, 2), new_states


def on_device(
    queries, key_vectors, values, gate_logits, decay_rates, norm_gain, pool_states, pool_entry
):
    req_dev, length, feature_width = queries.shape
    head_count = decay_rates.shape[0]
    head_size = pool_states.shape[2]
    ranks = lax.axis_size("batch")
    rows = req_dev * length
    lead = -rows % TILE
    if (
        ranks > 1
        and ranks & (ranks - 1) == 0
        and feature_width % (ranks * head_size) == 0
        and pool_states.shape[0] == 1
        and head_size % LANES == 0
        and 0 < lead < min(rows, TILE)
        and rows <= LANES
        and plan_rows(rows)[0] + LANES <= plan_rows(rows)[2]
        and plan_rows(rows)[2] == 3 * plan_rows(rows)[0] - 2 * TILE
    ):
        return by_heads(
            ranks, queries, key_vectors, values, gate_logits, decay_rates, norm_gain, pool_states, pool_entry
        )
    entries = lax.all_gather(pool_entry, "batch", axis=0, tiled=True)
    spread = lax.all_to_all(pool_states, "batch", split_axis=1, concat_axis=0, tiled=True)
    chosen = jnp.take(spread, entries, axis=0)
    resumed = lax.all_to_all(chosen, "batch", split_axis=0, concat_axis=1, tiled=True)
    resumed = resumed.reshape(req_dev, head_count, head_size, head_size)
    shaped = (req_dev, length, head_count, head_size)
    attended, updated = attend(
        queries.reshape(shaped),
        key_vectors.reshape(shaped),
        values.reshape(shaped),
        resumed,
        decay_rates,
    )
    attended = attended.reshape(req_dev, length, feature_width)
    local_states = updated.astype(jnp.bfloat16).reshape(req_dev, feature_width, head_size)
    new_states = lax.all_to_all(local_states, "batch", split_axis=1, concat_axis=0, tiled=True)
    mixed = finish_output(attended, gate_logits, norm_gain)
    return (mixed, new_states)


def solution(mesh):
    placed = (
        P(("groups", "batch"), None, None),
        P(("groups", "batch"), None, None),
        P(("groups", "batch"), None, None),
        P(("groups", "batch"), None, None),
        P(),
        P(),
        P(("groups", "batch"), None, None),
        P(("groups", "batch")),
    )
    return jax.shard_map(
        on_device,
        mesh=mesh,
        in_specs=placed,
        out_specs=(P(("groups", "batch"), None, None), P("groups", "batch", None)),
        check_vma=False,
    )
```

```python
import functools
import math

import jax
import jax.numpy as jnp
from jax import lax
from jax.experimental import pallas as pl
from jax.experimental.pallas import tpu as pltpu
from jax.sharding import PartitionSpec as P


def finish_output(attended, gate_logits, norm_gain):
    mean_square = jnp.mean(attended * attended, axis=-1, keepdims=True)
    scaled = attended * lax.rsqrt(mean_square + 1e-05) * norm_gain
    return (scaled * jax.nn.sigmoid(gate_logits.astype(jnp.float32))).astype(jnp.bfloat16)


def attend(query_part, key_part, value_part, resumed, rates_here):
    length = query_part.shape[1]
    highest = lax.Precision.HIGHEST
    positions = jnp.arange(1, length + 1).astype(jnp.float32)
    decay_now = jnp.exp(-positions[:, None] * rates_here[None, :])
    from_state = jnp.einsum(
        "rtgd,rgde->rtge", query_part, resumed, preferred_element_type=jnp.float32
    )
    from_state = from_state * decay_now[None, :, :, None]
    key_wide = key_part.astype(jnp.float32)
    value_wide = value_part.astype(jnp.float32)
    distance = positions[:, None] - positions[None, :]
    decay_pair = jnp.where(
        (distance >= 0.0)[:, :, None],
        jnp.exp(-jnp.maximum(distance, 0.0)[:, :, None] * rates_here),
        0.0,
    )
    scores = (
        jnp.einsum("rtgd,rsgd->rtsg", query_part, key_part, preferred_element_type=jnp.float32)
        * decay_pair[None]
    )
    in_block = jnp.einsum("rtsg,rsge->rtge", scores, value_wide, precision=highest)
    tail_decay = jnp.exp(-(float(length) - positions)[:, None] * rates_here[None, :])
    weighted_keys = key_wide * tail_decay[None, :, :, None]
    updated = jnp.exp(-float(length) * rates_here)[None, :, None, None] * resumed.astype(
        jnp.float32
    )
    updated = updated + jnp.einsum("rsgd,rsge->rgde", weighted_keys, value_wide, precision=highest)
    return (from_state + in_block, updated)


MESH = pl.DeviceIdType.MESH
TILE = 16
LANES = 128
CODE_TOP = 32000.0


def round_up(count, unit):
    return -(-count // unit) * unit


def plan_rows(rows):
    padded = round_up(rows, TILE)
    lead = padded - rows
    moved = round_up(padded + rows + rows - lead, TILE)
    return padded, lead, moved


def heads_kernel(
    dims,
    entry_ref,
    rates_ref,
    gain_ref,
    query_ref,
    key_ref,
    value_ref,
    gate_ref,
    pool_ref,
    mixed_ref,
    new_ref,
    staged,
    entry_mine,
    entry_all,
    entry_smem,
    packed,
    block_all,
    pool_all,
    pool_now,
    att_out,
    att_in,
    att_wide,
    gated,
    decay_now,
    decay_pair,
    decay_tail,
    entry_sems,
    pool_sems,
    block_sems,
    att_sems,
    state_sems,
    local_sems,
):
    n, reqs, length, heads, head = dims
    rows = reqs * length
    padded, lead, moved = plan_rows(rows)
    part = heads * head
    width = n * part
    shift = TILE - lead
    f32, bf16 = jnp.float32, jnp.bfloat16
    me = lax.axis_index("batch")

    def partner(i):
        step = (i % 2) * (n // 2) + i // 2
        peer = 0
        bit = 1
        while bit < n:
            peer = peer + ((me // bit + step // bit) % 2) * bit
            bit *= 2
        return peer

    barrier = pltpu.get_barrier_semaphore()

    def greet(i, carry):
        pl.semaphore_signal(barrier, inc=1, device_id={"batch": partner(i)}, device_id_type=MESH)
        return carry

    lax.fori_loop(1, n, greet, 0)

    lane = lax.broadcasted_iota(jnp.int32, (8, LANES), 1)
    mine = jnp.zeros((8, LANES), jnp.int32)
    for r in range(reqs):
        mine = jnp.where(lane == r, entry_ref[r], mine)
    entry_mine[...] = mine
    entry_all[me] = mine

    def remote(src, dst, send_sem, recv_sem, peer):
        return pltpu.make_async_remote_copy(
            src_ref=src,
            dst_ref=dst,
            send_sem=send_sem,
            recv_sem=recv_sem,
            device_id={"batch": peer},
            device_id_type=MESH,
        )

    def pool_rows(h, peer):
        return pool_ref.at[0, pl.ds(pl.multiple_of(peer * part + h * head, head), head), :]

    def entry_copy(peer, slot):
        return remote(
            entry_mine, entry_all.at[slot], entry_sems.at[0, peer], entry_sems.at[1, slot], peer
        )

    def pool_copy(h, peer, slot):
        return remote(
            pool_rows(h, peer),
            pool_all.at[h, slot],
            pool_sems.at[h, 0, peer],
            pool_sems.at[h, 1, slot],
            peer,
        )

    def block_copy(h, peer, slot):
        return remote(
            packed.at[h, peer],
            block_all.at[h, slot],
            block_sems.at[h, 0, peer],
            block_sems.at[h, 1, slot],
            peer,
        )

    def att_copy(h, peer, slot):
        return remote(
            att_out.at[h, peer],
            att_in.at[h, slot],
            att_sems.at[h, 0, peer],
            att_sems.at[h, 1, slot],
            peer,
        )

    def own_pool(h):
        return pltpu.make_async_copy(pool_rows(h, me), pool_all.at[h, me], local_sems.at[0, h])

    def own_att(h):
        return pltpu.make_async_copy(att_out.at[h, me], att_in.at[h, me], local_sems.at[1, h])

    def states_copy(h, peer):
        return pltpu.make_async_copy(
            staged.at[h, peer],
            new_ref.at[
                pl.ds(peer * reqs, reqs), pl.ds(pl.multiple_of(h * head, head), head), :
            ],
            state_sems.at[h, peer],
        )

    def block_of(h, peer):
        cols = pl.ds(pl.multiple_of(peer * part + h * head, head), head)
        key = key_ref[0:rows, cols].astype(f32)
        query = query_ref[0:rows, cols].astype(f32)
        value = value_ref[0:rows, cols].astype(f32)
        gap = jnp.zeros((moved - 3 * rows, head), f32)
        return jnp.concatenate([key, query[:lead], value, query[lead:], gap], axis=0).astype(bf16)

    def send_pool(h):
        def body(i, carry):
            pool_copy(h, partner(i), me).start()
            return carry

        lax.fori_loop(1, n, body, 0)
        own_pool(h).start()

    def pack_block(h, peer):
        packed[h, peer] = block_of(h, peer)

    def send_block(h, ready):
        def body(i, carry):
            peer = partner(i)
            if not ready:
                pack_block(h, peer)
            block_copy(h, peer, me).start()
            return carry

        lax.fori_loop(1, n, body, 0)
        block_all[h, me] = block_of(h, me)

    def pack_first(i, carry):
        pack_block(0, partner(i))
        return carry

    lax.fori_loop(1, n, pack_first, 0)

    def send_entries(i, carry):
        entry_copy(partner(i), me).start()
        return carry

    pl.semaphore_wait(barrier, n - 1)
    lax.fori_loop(1, n, send_entries, 0)
    for h in range(heads):
        send_pool(h)
        send_block(h, h == 0)

    def time_of(index):
        return (index // reqs + 1).astype(f32)

    def query_index(shape):
        row = lax.broadcasted_iota(jnp.int32, shape, 0)
        return jnp.maximum(jnp.where(row < TILE, row - shift, row - 2 * shift), 0)

    row_q = query_index((padded, head))
    row_k = lax.broadcasted_iota(jnp.int32, (padded, head), 0)
    pair_q = query_index((padded, LANES))
    pair_k = lax.broadcasted_iota(jnp.int32, (padded, LANES), 1)
    distance = time_of(pair_q) - time_of(pair_k)
    keep = (distance >= 0.0) & (pair_q % reqs == pair_k % reqs) & (pair_k < rows)
    for h in range(heads):
        rate = rates_ref[me * heads + h]
        decay_now[h] = jnp.exp(-time_of(row_q) * rate)
        decay_pair[h] = jnp.where(keep, jnp.exp(-jnp.maximum(distance, 0.0) * rate), 0.0)
        tail = jnp.exp(-jnp.maximum(float(length) - time_of(row_k), 0.0) * rate)
        for r in range(reqs):
            decay_tail[h, r] = jnp.where((row_k < rows) & (row_k % reqs == r), tail, 0.0)

    def prepare_gate(j, carry):
        at = pl.ds(pl.multiple_of(j * part, part), part)
        gated[:, at] = gain_ref[:, at] * jax.nn.sigmoid(gate_ref[0:rows, at].astype(f32))
        return carry

    lax.fori_loop(0, n, prepare_gate, 0)

    def wait_entries(i, carry):
        peer = partner(i)
        entry_copy(peer, peer).wait_recv()
        return carry

    lax.fori_loop(1, n, wait_entries, 0)
    listing = pltpu.make_async_copy(entry_all, entry_smem, local_sems.at[2, 0])
    listing.start()
    listing.wait()

    def split(wide):
        high = wide.astype(bf16)
        return high, (wide - high.astype(f32)).astype(bf16)

    def dot(a, b, dims):
        return lax.dot_general(a, b, (dims, ((), ())), preferred_element_type=f32)

    code_row = lax.broadcasted_iota(jnp.int32, (padded, head), 0)
    code_col = lax.broadcasted_iota(jnp.int32, (padded, head), 1)

    def encode(wide):
        size = jnp.abs(wide)
        power = jnp.ceil(jnp.log2(jnp.maximum(jnp.max(size, axis=1, keepdims=True), 1e-30)))
        root = jnp.sqrt(size * jnp.exp2(-power)) * CODE_TOP
        code = jnp.where(wide < 0.0, -root, root)
        powers = jnp.sum(jnp.where(code_row == code_col, power, 0.0), axis=0, keepdims=True)
        code = jnp.where(code_row == rows, powers, code)
        return jnp.round(code).astype(jnp.int32).astype(jnp.int16)

    def decode(code):
        wide = code.astype(jnp.int32).astype(f32)
        powers = jnp.where(code_row == code_col, wide[rows : rows + 1], 0.0)
        power = jnp.exp2(jnp.sum(powers, axis=1, keepdims=True)) * (1.0 / (CODE_TOP * CODE_TOP))
        return (wide * jnp.abs(wide) * power)[0:rows]

    def work(h, peer):
        starts = [pool_now[entry_smem[peer, 0, r]] for r in range(reqs)]
        key = block_all[h, peer, 0:padded]
        value = block_all[h, peer, padded : 2 * padded]
        query = jnp.concatenate(
            [block_all[h, peer, padded - TILE : padded], block_all[h, peer, 2 * padded - TILE : moved]],
            axis=0,
        )
        from_each = dot(query, jnp.concatenate(starts, axis=1), ((1,), (0,)))
        from_state = from_each[:, 0:head]
        for r in range(1, reqs):
            from_state = jnp.where(
                row_q % reqs == r, from_each[:, r * head : (r + 1) * head], from_state
            )
        scores = dot(query, block_all[h, peer, 0:LANES], ((1,), (1,))) * decay_pair[h]
        value_long = block_all[h, peer, padded : padded + LANES]
        attended = from_state * decay_now[h] + dot(
            jnp.concatenate(split(scores), axis=1),
            jnp.concatenate([value_long, value_long], axis=0),
            ((1,), (0,)),
        )
        att_out[h, peer] = encode(
            jnp.concatenate(
                [
                    attended[shift:TILE],
                    attended[TILE + shift : 2 * shift + rows],
                    jnp.zeros((padded - rows, head), f32),
                ],
                axis=0,
            )
        )
        value_wide = value.astype(f32)
        weighted = jnp.concatenate([value_wide * decay_tail[h, r] for r in range(reqs)], axis=1)
        added = dot(
            jnp.concatenate([key, key], axis=0),
            jnp.concatenate(split(weighted), axis=0),
            ((0,), (0,)),
        )
        fade = jnp.exp(jnp.full((8, head), -float(length), f32) * rates_ref[me * heads + h])[0:1]
        for r in range(reqs):
            staged[h, peer, r] = (
                fade * starts[r].astype(f32) + added[:, r * head : (r + 1) * head]
            ).astype(bf16)

    unroll = math.gcd(n, 4)

    def each_head(h, carry):
        def take_pool(i, inner):
            peer = partner(i)
            pool_copy(h, peer, peer).wait_recv()
            pool_now[peer] = pool_all[h, peer]
            return inner

        own_pool(h).wait()
        pool_now[me] = pool_all[h, me]
        lax.fori_loop(1, n, take_pool, 0)

        def each_group(g, inner):
            for u in range(unroll):
                i = g * unroll + u
                peer = partner(i)

                @pl.when(i > 0)
                def _():
                    block_copy(h, peer, peer).wait_recv()

            for u in range(unroll):
                work(h, partner(g * unroll + u))
            for u in range(unroll):
                i = g * unroll + u
                peer = partner(i)

                @pl.when(i > 0)
                def _():
                    att_copy(h, peer, me).start()

                @pl.when(i == 0)
                def _():
                    own_att(h).start()

                states_copy(h, peer).start()
            return inner

        lax.fori_loop(0, n // unroll, each_group, 0)
        return carry

    lax.fori_loop(0, heads, each_head, 0)

    def gather_head(h, total):
        own_att(h).wait()
        own = decode(att_in[h, me])
        att_wide[h, me] = own

        def gather(i, inner):
            peer = partner(i)
            att_copy(h, peer, peer).wait_recv()
            here = decode(att_in[h, peer])
            att_wide[h, peer] = here
            return inner + here * here

        return lax.fori_loop(1, n, gather, total + own * own)

    squares = lax.fori_loop(0, heads, gather_head, jnp.zeros((rows, head), f32))
    squares = jnp.sum(squares, axis=1, keepdims=True)
    scale = lax.rsqrt(squares * (1.0 / width) + 1e-05)

    def finish(j, carry):
        for h in range(heads):
            at = pl.ds(pl.multiple_of(j * part + h * head, head), head)
            mixed_ref[:, at] = (att_wide[h, j] * scale * gated[:, at]).astype(bf16)
        return carry

    lax.fori_loop(0, n, finish, 0)

    def settle(i, carry):
        peer = partner(i)
        entry_copy(peer, me).wait_send()
        for h in range(heads):
            pool_copy(h, peer, me).wait_send()
            block_copy(h, peer, me).wait_send()
            att_copy(h, peer, me).wait_send()
            states_copy(h, peer).wait()
        return carry

    lax.fori_loop(1, n, settle, 0)
    for h in range(heads):
        states_copy(h, me).wait()


def by_heads(
    n, queries, key_vectors, values, gate_logits, decay_rates, norm_gain, pool_states, pool_entry
):
    reqs, length, width = queries.shape
    head = pool_states.shape[2]
    part = width // n
    heads = part // head
    rows = reqs * length
    padded, lead, moved = plan_rows(rows)
    flat = [
        item.transpose(1, 0, 2).reshape(rows, width)
        for item in (queries, key_vectors, values, gate_logits)
    ]
    f32, bf16 = jnp.float32, jnp.bfloat16
    vmem = pl.BlockSpec(memory_space=pltpu.VMEM)
    smem = pl.BlockSpec(memory_space=pltpu.SMEM)
    anywhere = pl.BlockSpec(memory_space=pl.ANY)
    mixed, new_states = pl.pallas_call(
        functools.partial(heads_kernel, (n, reqs, length, heads, head)),
        out_shape=(
            jax.ShapeDtypeStruct((rows, width), bf16),
            jax.ShapeDtypeStruct((n * reqs, part, head), bf16),
        ),
        in_specs=[smem, smem, vmem, vmem, vmem, vmem, vmem, anywhere],
        out_specs=(vmem, anywhere),
        scratch_shapes=[
            pltpu.VMEM((heads, n, reqs, head, head), bf16),
            pltpu.VMEM((8, LANES), jnp.int32),
            pltpu.VMEM((n, 8, LANES), jnp.int32),
            pltpu.SMEM((n, 8, LANES), jnp.int32),
            pltpu.VMEM((heads, n, moved, head), bf16),
            pltpu.VMEM((heads, n, moved, head), bf16),
            pltpu.VMEM((heads, n, head, head), bf16),
            pltpu.VMEM((n, head, head), bf16),
            pltpu.VMEM((heads, n, padded, head), jnp.int16),
            pltpu.VMEM((heads, n, padded, head), jnp.int16),
            pltpu.VMEM((heads, n, rows, head), f32),
            pltpu.VMEM((rows, width), f32),
            pltpu.VMEM((heads, padded, head), f32),
            pltpu.VMEM((heads, padded, LANES), f32),
            pltpu.VMEM((heads, reqs, padded, head), f32),
            pltpu.SemaphoreType.DMA((2, n)),
            pltpu.SemaphoreType.DMA((heads, 2, n)),
            pltpu.SemaphoreType.DMA((heads, 2, n)),
            pltpu.SemaphoreType.DMA((heads, 2, n)),
            pltpu.SemaphoreType.DMA((heads, n)),
            pltpu.SemaphoreType.DMA((3, heads)),
        ],
        compiler_params=pltpu.CompilerParams(
            collective_id=0, has_side_effects=True, vmem_limit_bytes=38 * 1024 * 1024
        ),
    )(pool_entry, decay_rates, norm_gain.reshape(1, width), *flat, pool_states)
    return mixed.reshape(length, reqs, width).transpose(1, 0, 2), new_states


def on_device(
    queries, key_vectors, values, gate_logits, decay_rates, norm_gain, pool_states, pool_entry
):
    req_dev, length, feature_width = queries.shape
    head_count = decay_rates.shape[0]
    head_size = pool_states.shape[2]
    ranks = lax.axis_size("batch")
    rows = req_dev * length
    lead = -rows % TILE
    if (
        ranks > 1
        and ranks & (ranks - 1) == 0
        and feature_width % (ranks * head_size) == 0
        and pool_states.shape[0] == 1
        and head_size % LANES == 0
        and 0 < lead < min(rows, TILE)
        and rows <= LANES
        and plan_rows(rows)[0] + LANES <= plan_rows(rows)[2]
        and plan_rows(rows)[2] == 3 * plan_rows(rows)[0] - 2 * TILE
    ):
        return by_heads(
            ranks, queries, key_vectors, values, gate_logits, decay_rates, norm_gain, pool_states, pool_entry
        )
    entries = lax.all_gather(pool_entry, "batch", axis=0, tiled=True)
    spread = lax.all_to_all(pool_states, "batch", split_axis=1, concat_axis=0, tiled=True)
    chosen = jnp.take(spread, entries, axis=0)
    resumed = lax.all_to_all(chosen, "batch", split_axis=0, concat_axis=1, tiled=True)
    resumed = resumed.reshape(req_dev, head_count, head_size, head_size)
    shaped = (req_dev, length, head_count, head_size)
    attended, updated = attend(
        queries.reshape(shaped),
        key_vectors.reshape(shaped),
        values.reshape(shaped),
        resumed,
        decay_rates,
    )
    attended = attended.reshape(req_dev, length, feature_width)
    local_states = updated.astype(jnp.bfloat16).reshape(req_dev, feature_width, head_size)
    new_states = lax.all_to_all(local_states, "batch", split_axis=1, concat_axis=0, tiled=True)
    mixed = finish_output(attended, gate_logits, norm_gain)
    return (mixed, new_states)


def solution(mesh):
    placed = (
        P(("groups", "batch"), None, None),
        P(("groups", "batch"), None, None),
        P(("groups", "batch"), None, None),
        P(("groups", "batch"), None, None),
        P(),
        P(),
        P(("groups", "batch"), None, None),
        P(("groups", "batch")),
    )
    return jax.shard_map(
        on_device,
        mesh=mesh,
        in_specs=placed,
        out_specs=(P(("groups", "batch"), None, None), P("groups", "batch", None)),
        check_vma=False,
    )
```

```python
import functools
import math

import jax
import jax.numpy as jnp
from jax import lax
from jax.experimental import pallas as pl
from jax.experimental.pallas import tpu as pltpu
from jax.sharding import PartitionSpec as P


def finish_output(attended, gate_logits, norm_gain):
    mean_square = jnp.mean(attended * attended, axis=-1, keepdims=True)
    scaled = attended * lax.rsqrt(mean_square + 1e-05) * norm_gain
    return (scaled * jax.nn.sigmoid(gate_logits.astype(jnp.float32))).astype(jnp.bfloat16)


def attend(query_part, key_part, value_part, resumed, rates_here):
    length = query_part.shape[1]
    highest = lax.Precision.HIGHEST
    positions = jnp.arange(1, length + 1).astype(jnp.float32)
    decay_now = jnp.exp(-positions[:, None] * rates_here[None, :])
    from_state = jnp.einsum(
        "rtgd,rgde->rtge", query_part, resumed, preferred_element_type=jnp.float32
    )
    from_state = from_state * decay_now[None, :, :, None]
    key_wide = key_part.astype(jnp.float32)
    value_wide = value_part.astype(jnp.float32)
    distance = positions[:, None] - positions[None, :]
    decay_pair = jnp.where(
        (distance >= 0.0)[:, :, None],
        jnp.exp(-jnp.maximum(distance, 0.0)[:, :, None] * rates_here),
        0.0,
    )
    scores = (
        jnp.einsum("rtgd,rsgd->rtsg", query_part, key_part, preferred_element_type=jnp.float32)
        * decay_pair[None]
    )
    in_block = jnp.einsum("rtsg,rsge->rtge", scores, value_wide, precision=highest)
    tail_decay = jnp.exp(-(float(length) - positions)[:, None] * rates_here[None, :])
    weighted_keys = key_wide * tail_decay[None, :, :, None]
    updated = jnp.exp(-float(length) * rates_here)[None, :, None, None] * resumed.astype(
        jnp.float32
    )
    updated = updated + jnp.einsum("rsgd,rsge->rgde", weighted_keys, value_wide, precision=highest)
    return (from_state + in_block, updated)


MESH = pl.DeviceIdType.MESH
TILE = 16
LANES = 128
CODE_TOP = 32000.0


def round_up(count, unit):
    return -(-count // unit) * unit


def plan_rows(rows):
    padded = round_up(rows, TILE)
    lead = padded - rows
    moved = round_up(padded + rows + rows - lead, TILE)
    return padded, lead, moved


def heads_kernel(
    dims,
    entry_ref,
    rates_ref,
    gain_ref,
    query_ref,
    key_ref,
    value_ref,
    gate_ref,
    pool_ref,
    mixed_ref,
    new_ref,
    staged,
    entry_mine,
    entry_all,
    entry_smem,
    packed,
    block_all,
    pool_all,
    pool_now,
    att_out,
    att_in,
    att_wide,
    gated,
    decay_now,
    decay_pair,
    decay_tail,
    entry_sems,
    pool_sems,
    block_sems,
    att_sems,
    state_sems,
    local_sems,
):
    n, reqs, length, heads, head = dims
    rows = reqs * length
    padded, lead, moved = plan_rows(rows)
    part = heads * head
    width = n * part
    shift = TILE - lead
    f32, bf16 = jnp.float32, jnp.bfloat16
    me = lax.axis_index("batch")

    def partner(i):
        step = (i % 2) * (n // 2) + i // 2
        peer = 0
        bit = 1
        while bit < n:
            peer = peer + ((me // bit + step // bit) % 2) * bit
            bit *= 2
        return peer

    barrier = pltpu.get_barrier_semaphore()

    def greet(i, carry):
        pl.semaphore_signal(barrier, inc=1, device_id={"batch": partner(i)}, device_id_type=MESH)
        return carry

    lax.fori_loop(1, n, greet, 0)

    lane = lax.broadcasted_iota(jnp.int32, (8, LANES), 1)
    mine = jnp.zeros((8, LANES), jnp.int32)
    for r in range(reqs):
        mine = jnp.where(lane == r, entry_ref[r], mine)
    entry_mine[...] = mine
    entry_all[me] = mine

    def remote(src, dst, send_sem, recv_sem, peer):
        return pltpu.make_async_remote_copy(
            src_ref=src,
            dst_ref=dst,
            send_sem=send_sem,
            recv_sem=recv_sem,
            device_id={"batch": peer},
            device_id_type=MESH,
        )

    def pool_rows(h, peer):
        return pool_ref.at[0, pl.ds(pl.multiple_of(peer * part + h * head, head), head), :]

    def entry_copy(peer, slot):
        return remote(
            entry_mine, entry_all.at[slot], entry_sems.at[0, peer], entry_sems.at[1, slot], peer
        )

    def pool_copy(h, peer, slot):
        return remote(
            pool_rows(h, peer),
            pool_all.at[h, slot],
            pool_sems.at[h, 0, peer],
            pool_sems.at[h, 1, slot],
            peer,
        )

    def block_copy(h, peer, slot):
        return remote(
            packed.at[h, peer],
            block_all.at[h, slot],
            block_sems.at[h, 0, peer],
            block_sems.at[h, 1, slot],
            peer,
        )

    def att_copy(h, peer, slot):
        return remote(
            att_out.at[h, peer],
            att_in.at[h, slot],
            att_sems.at[h, 0, peer],
            att_sems.at[h, 1, slot],
            peer,
        )

    def own_pool(h):
        return pltpu.make_async_copy(pool_rows(h, me), pool_all.at[h, me], local_sems.at[0, h])

    def own_att(h):
        return pltpu.make_async_copy(att_out.at[h, me], att_in.at[h, me], local_sems.at[1, h])

    def states_copy(h, peer):
        return pltpu.make_async_copy(
            staged.at[h, peer],
            new_ref.at[
                pl.ds(peer * reqs, reqs), pl.ds(pl.multiple_of(h * head, head), head), :
            ],
            state_sems.at[h, peer],
        )

    def block_of(h, peer):
        cols = pl.ds(pl.multiple_of(peer * part + h * head, head), head)
        key = key_ref[0:rows, cols].astype(f32)
        query = query_ref[0:rows, cols].astype(f32)
        value = value_ref[0:rows, cols].astype(f32)
        gap = jnp.zeros((moved - 3 * rows, head), f32)
        return jnp.concatenate([key, query[:lead], value, query[lead:], gap], axis=0).astype(bf16)

    def send_pool(h):
        def body(i, carry):
            pool_copy(h, partner(i), me).start()
            return carry

        lax.fori_loop(1, n, body, 0)
        own_pool(h).start()

    def pack_block(h, peer):
        packed[h, peer] = block_of(h, peer)

    def send_block(h, first, last, ready):
        def body(i, carry):
            @pl.when(i > 0)
            def _():
                peer = partner(i)
                if not ready:
                    pack_block(h, peer)
                block_copy(h, peer, me).start()

            return carry

        lax.fori_loop(first, last, body, 0)

    def pack_first(i, carry):
        pack_block(0, partner(i))
        return carry

    lax.fori_loop(1, n, pack_first, 0)

    def send_entries(i, carry):
        entry_copy(partner(i), me).start()
        return carry

    pl.semaphore_wait(barrier, n - 1)
    lax.fori_loop(1, n, send_entries, 0)
    send_pool(0)
    send_block(0, 0, n, True)
    for h in range(heads):
        block_all[h, me] = block_of(h, me)

    def time_of(index):
        return (index // reqs + 1).astype(f32)

    def query_index(shape):
        row = lax.broadcasted_iota(jnp.int32, shape, 0)
        return jnp.maximum(jnp.where(row < TILE, row - shift, row - 2 * shift), 0)

    row_q = query_index((padded, head))
    row_k = lax.broadcasted_iota(jnp.int32, (padded, head), 0)
    pair_q = query_index((padded, LANES))
    pair_k = lax.broadcasted_iota(jnp.int32, (padded, LANES), 1)
    distance = time_of(pair_q) - time_of(pair_k)
    keep = (distance >= 0.0) & (pair_q % reqs == pair_k % reqs) & (pair_k < rows)
    for h in range(heads):
        rate = rates_ref[me * heads + h]
        decay_now[h] = jnp.exp(-time_of(row_q) * rate)
        decay_pair[h] = jnp.where(keep, jnp.exp(-jnp.maximum(distance, 0.0) * rate), 0.0)
        tail = jnp.exp(-jnp.maximum(float(length) - time_of(row_k), 0.0) * rate)
        for r in range(reqs):
            decay_tail[h, r] = jnp.where((row_k < rows) & (row_k % reqs == r), tail, 0.0)

    def prepare_gate(j, carry):
        at = pl.ds(pl.multiple_of(j * part, part), part)
        gated[:, at] = gain_ref[:, at] * jax.nn.sigmoid(gate_ref[0:rows, at].astype(f32))
        return carry

    lax.fori_loop(0, n, prepare_gate, 0)

    def wait_entries(i, carry):
        peer = partner(i)
        entry_copy(peer, peer).wait_recv()
        return carry

    lax.fori_loop(1, n, wait_entries, 0)
    listing = pltpu.make_async_copy(entry_all, entry_smem, local_sems.at[2, 0])
    listing.start()
    listing.wait()

    def split(wide):
        high = wide.astype(bf16)
        return high, (wide - high.astype(f32)).astype(bf16)

    def dot(a, b, dims):
        return lax.dot_general(a, b, (dims, ((), ())), preferred_element_type=f32)

    code_row = lax.broadcasted_iota(jnp.int32, (padded, head), 0)
    code_col = lax.broadcasted_iota(jnp.int32, (padded, head), 1)

    def encode(wide):
        size = jnp.abs(wide)
        power = jnp.ceil(jnp.log2(jnp.maximum(jnp.max(size, axis=1, keepdims=True), 1e-30)))
        root = jnp.sqrt(size * jnp.exp2(-power)) * CODE_TOP
        code = jnp.where(wide < 0.0, -root, root)
        powers = jnp.sum(jnp.where(code_row == code_col, power, 0.0), axis=0, keepdims=True)
        code = jnp.where(code_row == rows, powers, code)
        return jnp.round(code).astype(jnp.int32).astype(jnp.int16)

    def decode(code):
        wide = code.astype(jnp.int32).astype(f32)
        powers = jnp.where(code_row == code_col, wide[rows : rows + 1], 0.0)
        power = jnp.exp2(jnp.sum(powers, axis=1, keepdims=True)) * (1.0 / (CODE_TOP * CODE_TOP))
        return (wide * jnp.abs(wide) * power)[0:rows]

    def work(h, peer):
        starts = [pool_now[entry_smem[peer, 0, r]] for r in range(reqs)]
        key = block_all[h, peer, 0:padded]
        value = block_all[h, peer, padded : 2 * padded]
        query = jnp.concatenate(
            [block_all[h, peer, padded - TILE : padded], block_all[h, peer, 2 * padded - TILE : moved]],
            axis=0,
        )
        from_each = dot(query, jnp.concatenate(starts, axis=1), ((1,), (0,)))
        from_state = from_each[:, 0:head]
        for r in range(1, reqs):
            from_state = jnp.where(
                row_q % reqs == r, from_each[:, r * head : (r + 1) * head], from_state
            )
        scores = dot(query, block_all[h, peer, 0:LANES], ((1,), (1,))) * decay_pair[h]
        value_long = block_all[h, peer, padded : padded + LANES]
        attended = from_state * decay_now[h] + dot(
            jnp.concatenate(split(scores), axis=1),
            jnp.concatenate([value_long, value_long], axis=0),
            ((1,), (0,)),
        )
        att_out[h, peer] = encode(
            jnp.concatenate(
                [
                    attended[shift:TILE],
                    attended[TILE + shift : 2 * shift + rows],
                    jnp.zeros((padded - rows, head), f32),
                ],
                axis=0,
            )
        )
        value_wide = value.astype(f32)
        weighted = jnp.concatenate([value_wide * decay_tail[h, r] for r in range(reqs)], axis=1)
        added = dot(
            jnp.concatenate([key, key], axis=0),
            jnp.concatenate(split(weighted), axis=0),
            ((0,), (0,)),
        )
        fade = jnp.exp(jnp.full((8, head), -float(length), f32) * rates_ref[me * heads + h])[0:1]
        for r in range(reqs):
            staged[h, peer, r] = (
                fade * starts[r].astype(f32) + added[:, r * head : (r + 1) * head]
            ).astype(bf16)

    unroll = math.gcd(n, 4)

    def each_head(h, carry):
        def take_pool(i, inner):
            peer = partner(i)
            pool_copy(h, peer, peer).wait_recv()
            pool_now[peer] = pool_all[h, peer]
            return inner

        own_pool(h).wait()
        pool_now[me] = pool_all[h, me]
        lax.fori_loop(1, n, take_pool, 0)

        @pl.when(h + 1 < heads)
        def _():
            send_pool(h + 1)

        def each_group(g, inner):
            for u in range(unroll):
                i = g * unroll + u
                peer = partner(i)

                @pl.when(i > 0)
                def _():
                    block_copy(h, peer, peer).wait_recv()

            @pl.when(h + 1 < heads)
            def _():
                send_block(h + 1, g * unroll, (g + 1) * unroll, False)

            for u in range(unroll):
                work(h, partner(g * unroll + u))
            for u in range(unroll):
                i = g * unroll + u
                peer = partner(i)

                @pl.when(i > 0)
                def _():
                    att_copy(h, peer, me).start()

                @pl.when(i == 0)
                def _():
                    own_att(h).start()

                states_copy(h, peer).start()

            return inner

        lax.fori_loop(0, n // unroll, each_group, 0)
        return carry

    lax.fori_loop(0, heads, each_head, 0)

    def gather_head(h, total):
        own_att(h).wait()
        own = decode(att_in[h, me])
        att_wide[h, me] = own

        def gather(i, inner):
            peer = partner(i)
            att_copy(h, peer, peer).wait_recv()
            here = decode(att_in[h, peer])
            att_wide[h, peer] = here
            return inner + here * here

        return lax.fori_loop(1, n, gather, total + own * own)

    squares = lax.fori_loop(0, heads, gather_head, jnp.zeros((rows, head), f32))
    squares = jnp.sum(squares, axis=1, keepdims=True)
    scale = lax.rsqrt(squares * (1.0 / width) + 1e-05)

    def finish(j, carry):
        for h in range(heads):
            at = pl.ds(pl.multiple_of(j * part + h * head, head), head)
            mixed_ref[:, at] = (att_wide[h, j] * scale * gated[:, at]).astype(bf16)
        return carry

    lax.fori_loop(0, n, finish, 0)

    def settle(i, carry):
        peer = partner(i)
        entry_copy(peer, me).wait_send()
        for h in range(heads):
            pool_copy(h, peer, me).wait_send()
            block_copy(h, peer, me).wait_send()
            att_copy(h, peer, me).wait_send()
            states_copy(h, peer).wait()
        return carry

    lax.fori_loop(1, n, settle, 0)
    for h in range(heads):
        states_copy(h, me).wait()


def by_heads(
    n, queries, key_vectors, values, gate_logits, decay_rates, norm_gain, pool_states, pool_entry
):
    reqs, length, width = queries.shape
    head = pool_states.shape[2]
    part = width // n
    heads = part // head
    rows = reqs * length
    padded, lead, moved = plan_rows(rows)
    flat = [
        item.transpose(1, 0, 2).reshape(rows, width)
        for item in (queries, key_vectors, values, gate_logits)
    ]
    f32, bf16 = jnp.float32, jnp.bfloat16
    vmem = pl.BlockSpec(memory_space=pltpu.VMEM)
    smem = pl.BlockSpec(memory_space=pltpu.SMEM)
    anywhere = pl.BlockSpec(memory_space=pl.ANY)
    mixed, new_states = pl.pallas_call(
        functools.partial(heads_kernel, (n, reqs, length, heads, head)),
        out_shape=(
            jax.ShapeDtypeStruct((rows, width), bf16),
            jax.ShapeDtypeStruct((n * reqs, part, head), bf16),
        ),
        in_specs=[smem, smem, vmem, vmem, vmem, vmem, vmem, anywhere],
        out_specs=(vmem, anywhere),
        scratch_shapes=[
            pltpu.VMEM((heads, n, reqs, head, head), bf16),
            pltpu.VMEM((8, LANES), jnp.int32),
            pltpu.VMEM((n, 8, LANES), jnp.int32),
            pltpu.SMEM((n, 8, LANES), jnp.int32),
            pltpu.VMEM((heads, n, moved, head), bf16),
            pltpu.VMEM((heads, n, moved, head), bf16),
            pltpu.VMEM((heads, n, head, head), bf16),
            pltpu.VMEM((n, head, head), bf16),
            pltpu.VMEM((heads, n, padded, head), jnp.int16),
            pltpu.VMEM((heads, n, padded, head), jnp.int16),
            pltpu.VMEM((heads, n, rows, head), f32),
            pltpu.VMEM((rows, width), f32),
            pltpu.VMEM((heads, padded, head), f32),
            pltpu.VMEM((heads, padded, LANES), f32),
            pltpu.VMEM((heads, reqs, padded, head), f32),
            pltpu.SemaphoreType.DMA((2, n)),
            pltpu.SemaphoreType.DMA((heads, 2, n)),
            pltpu.SemaphoreType.DMA((heads, 2, n)),
            pltpu.SemaphoreType.DMA((heads, 2, n)),
            pltpu.SemaphoreType.DMA((heads, n)),
            pltpu.SemaphoreType.DMA((3, heads)),
        ],
        compiler_params=pltpu.CompilerParams(
            collective_id=0, has_side_effects=True, vmem_limit_bytes=38 * 1024 * 1024
        ),
    )(pool_entry, decay_rates, norm_gain.reshape(1, width), *flat, pool_states)
    return mixed.reshape(length, reqs, width).transpose(1, 0, 2), new_states


def on_device(
    queries, key_vectors, values, gate_logits, decay_rates, norm_gain, pool_states, pool_entry
):
    req_dev, length, feature_width = queries.shape
    head_count = decay_rates.shape[0]
    head_size = pool_states.shape[2]
    ranks = lax.axis_size("batch")
    rows = req_dev * length
    lead = -rows % TILE
    if (
        ranks > 1
        and ranks & (ranks - 1) == 0
        and feature_width % (ranks * head_size) == 0
        and pool_states.shape[0] == 1
        and head_size % LANES == 0
        and 0 < lead < min(rows, TILE)
        and rows <= LANES
        and plan_rows(rows)[0] + LANES <= plan_rows(rows)[2]
        and plan_rows(rows)[2] == 3 * plan_rows(rows)[0] - 2 * TILE
    ):
        return by_heads(
            ranks, queries, key_vectors, values, gate_logits, decay_rates, norm_gain, pool_states, pool_entry
        )
    entries = lax.all_gather(pool_entry, "batch", axis=0, tiled=True)
    spread = lax.all_to_all(pool_states, "batch", split_axis=1, concat_axis=0, tiled=True)
    chosen = jnp.take(spread, entries, axis=0)
    resumed = lax.all_to_all(chosen, "batch", split_axis=0, concat_axis=1, tiled=True)
    resumed = resumed.reshape(req_dev, head_count, head_size, head_size)
    shaped = (req_dev, length, head_count, head_size)
    attended, updated = attend(
        queries.reshape(shaped),
        key_vectors.reshape(shaped),
        values.reshape(shaped),
        resumed,
        decay_rates,
    )
    attended = attended.reshape(req_dev, length, feature_width)
    local_states = updated.astype(jnp.bfloat16).reshape(req_dev, feature_width, head_size)
    new_states = lax.all_to_all(local_states, "batch", split_axis=1, concat_axis=0, tiled=True)
    mixed = finish_output(attended, gate_logits, norm_gain)
    return (mixed, new_states)


def solution(mesh):
    placed = (
        P(("groups", "batch"), None, None),
        P(("groups", "batch"), None, None),
        P(("groups", "batch"), None, None),
        P(("groups", "batch"), None, None),
        P(),
        P(),
        P(("groups", "batch"), None, None),
        P(("groups", "batch")),
    )
    return jax.shard_map(
        on_device,
        mesh=mesh,
        in_specs=placed,
        out_specs=(P(("groups", "batch"), None, None), P("groups", "batch", None)),
        check_vma=False,
    )
```

```python
import functools
import math

import jax
import jax.numpy as jnp
from jax import lax
from jax.experimental import pallas as pl
from jax.experimental.pallas import tpu as pltpu
from jax.sharding import PartitionSpec as P


def finish_output(attended, gate_logits, norm_gain):
    mean_square = jnp.mean(attended * attended, axis=-1, keepdims=True)
    scaled = attended * lax.rsqrt(mean_square + 1e-05) * norm_gain
    return (scaled * jax.nn.sigmoid(gate_logits.astype(jnp.float32))).astype(jnp.bfloat16)


def attend(query_part, key_part, value_part, resumed, rates_here):
    length = query_part.shape[1]
    highest = lax.Precision.HIGHEST
    positions = jnp.arange(1, length + 1).astype(jnp.float32)
    decay_now = jnp.exp(-positions[:, None] * rates_here[None, :])
    from_state = jnp.einsum(
        "rtgd,rgde->rtge", query_part, resumed, preferred_element_type=jnp.float32
    )
    from_state = from_state * decay_now[None, :, :, None]
    key_wide = key_part.astype(jnp.float32)
    value_wide = value_part.astype(jnp.float32)
    distance = positions[:, None] - positions[None, :]
    decay_pair = jnp.where(
        (distance >= 0.0)[:, :, None],
        jnp.exp(-jnp.maximum(distance, 0.0)[:, :, None] * rates_here),
        0.0,
    )
    scores = (
        jnp.einsum("rtgd,rsgd->rtsg", query_part, key_part, preferred_element_type=jnp.float32)
        * decay_pair[None]
    )
    in_block = jnp.einsum("rtsg,rsge->rtge", scores, value_wide, precision=highest)
    tail_decay = jnp.exp(-(float(length) - positions)[:, None] * rates_here[None, :])
    weighted_keys = key_wide * tail_decay[None, :, :, None]
    updated = jnp.exp(-float(length) * rates_here)[None, :, None, None] * resumed.astype(
        jnp.float32
    )
    updated = updated + jnp.einsum("rsgd,rsge->rgde", weighted_keys, value_wide, precision=highest)
    return (from_state + in_block, updated)


MESH = pl.DeviceIdType.MESH
TILE = 16
LANES = 128
CODE_TOP = 32000.0


def round_up(count, unit):
    return -(-count // unit) * unit


def plan_rows(rows):
    padded = round_up(rows, TILE)
    lead = padded - rows
    moved = round_up(padded + rows + rows - lead, TILE)
    return padded, lead, moved


def heads_kernel(
    dims,
    entry_ref,
    rates_ref,
    gain_ref,
    query_ref,
    key_ref,
    value_ref,
    gate_ref,
    pool_ref,
    mixed_ref,
    new_ref,
    staged,
    entry_mine,
    entry_all,
    entry_smem,
    packed,
    block_all,
    pool_all,
    pool_now,
    att_out,
    att_in,
    att_wide,
    gated,
    decay_now,
    decay_pair,
    decay_tail,
    entry_sems,
    pool_sems,
    block_sems,
    att_sems,
    state_sems,
    local_sems,
):
    n, reqs, length, heads, head = dims
    rows = reqs * length
    padded, lead, moved = plan_rows(rows)
    part = heads * head
    width = n * part
    shift = TILE - lead
    f32, bf16 = jnp.float32, jnp.bfloat16
    me = lax.axis_index("batch")

    def partner(i):
        step = (i % 2) * (n // 2) + i // 2
        peer = 0
        bit = 1
        while bit < n:
            peer = peer + ((me // bit + step // bit) % 2) * bit
            bit *= 2
        return peer

    barrier = pltpu.get_barrier_semaphore()

    def greet(i, carry):
        pl.semaphore_signal(barrier, inc=1, device_id={"batch": partner(i)}, device_id_type=MESH)
        return carry

    lax.fori_loop(1, n, greet, 0)

    lane = lax.broadcasted_iota(jnp.int32, (8, LANES), 1)
    mine = jnp.zeros((8, LANES), jnp.int32)
    for r in range(reqs):
        mine = jnp.where(lane == r, entry_ref[r], mine)
    entry_mine[...] = mine
    entry_all[me] = mine

    def remote(src, dst, send_sem, recv_sem, peer):
        return pltpu.make_async_remote_copy(
            src_ref=src,
            dst_ref=dst,
            send_sem=send_sem,
            recv_sem=recv_sem,
            device_id={"batch": peer},
            device_id_type=MESH,
        )

    def pool_rows(h, peer):
        return pool_ref.at[0, pl.ds(pl.multiple_of(peer * part + h * head, head), head), :]

    def entry_copy(peer, slot):
        return remote(
            entry_mine, entry_all.at[slot], entry_sems.at[0, peer], entry_sems.at[1, slot], peer
        )

    def pool_copy(h, peer, slot):
        return remote(
            pool_rows(h, peer),
            pool_all.at[h, slot],
            pool_sems.at[h, 0, peer],
            pool_sems.at[h, 1, slot],
            peer,
        )

    def block_copy(h, peer, slot):
        return remote(
            packed.at[h, peer],
            block_all.at[h, slot],
            block_sems.at[h, 0, peer],
            block_sems.at[h, 1, slot],
            peer,
        )

    def att_copy(h, peer, slot):
        return remote(
            att_out.at[h, peer],
            att_in.at[h, slot],
            att_sems.at[h, 0, peer],
            att_sems.at[h, 1, slot],
            peer,
        )

    def own_pool(h):
        return pltpu.make_async_copy(pool_rows(h, me), pool_all.at[h, me], local_sems.at[0, h])

    def own_att(h):
        return pltpu.make_async_copy(att_out.at[h, me], att_in.at[h, me], local_sems.at[1, h])

    def states_copy(h, peer):
        return pltpu.make_async_copy(
            staged.at[h, peer],
            new_ref.at[
                pl.ds(peer * reqs, reqs), pl.ds(pl.multiple_of(h * head, head), head), :
            ],
            state_sems.at[h, peer],
        )

    def block_of(h, peer):
        cols = pl.ds(pl.multiple_of(peer * part + h * head, head), head)
        key, query, value = (
            ref[:, :, cols].astype(f32).reshape(rows, head) for ref in (key_ref, query_ref, value_ref)
        )
        gap = jnp.zeros((moved - 3 * rows, head), f32)
        return jnp.concatenate([key, query[:lead], value, query[lead:], gap], axis=0).astype(bf16)

    def send_pool(h):
        def body(i, carry):
            pool_copy(h, partner(i), me).start()
            return carry

        lax.fori_loop(1, n, body, 0)
        own_pool(h).start()

    def pack_block(h, peer):
        packed[h, peer] = block_of(h, peer)

    def send_block(h, ready):
        def body(i, carry):
            peer = partner(i)
            if not ready:
                pack_block(h, peer)
            block_copy(h, peer, me).start()
            return carry

        lax.fori_loop(1, n, body, 0)
        block_all[h, me] = block_of(h, me)

    def pack_first(i, carry):
        pack_block(0, partner(i))
        return carry

    lax.fori_loop(1, n, pack_first, 0)

    def send_entries(i, carry):
        entry_copy(partner(i), me).start()
        return carry

    pl.semaphore_wait(barrier, n - 1)
    lax.fori_loop(1, n, send_entries, 0)
    for h in range(heads):
        send_pool(h)
        send_block(h, h == 0)

    def time_of(index):
        return (index // reqs + 1).astype(f32)

    def query_index(shape):
        row = lax.broadcasted_iota(jnp.int32, shape, 0)
        return jnp.maximum(jnp.where(row < TILE, row - shift, row - 2 * shift), 0)

    row_q = query_index((padded, head))
    row_k = lax.broadcasted_iota(jnp.int32, (padded, head), 0)
    pair_q = query_index((padded, LANES))
    pair_k = lax.broadcasted_iota(jnp.int32, (padded, LANES), 1)
    distance = time_of(pair_q) - time_of(pair_k)
    keep = (distance >= 0.0) & (pair_q % reqs == pair_k % reqs) & (pair_k < rows)
    for h in range(heads):
        rate = rates_ref[me * heads + h]
        decay_now[h] = jnp.exp(-time_of(row_q) * rate)
        decay_pair[h] = jnp.where(keep, jnp.exp(-jnp.maximum(distance, 0.0) * rate), 0.0)
        tail = jnp.exp(-jnp.maximum(float(length) - time_of(row_k), 0.0) * rate)
        for r in range(reqs):
            decay_tail[h, r] = jnp.where((row_k < rows) & (row_k % reqs == r), tail, 0.0)

    def prepare_gate(j, carry):
        at = pl.ds(pl.multiple_of(j * part, part), part)
        gate = gate_ref[:, :, at].astype(f32).reshape(rows, part)
        gated[:, at] = gain_ref[:, at] * jax.nn.sigmoid(gate)
        return carry

    lax.fori_loop(0, n, prepare_gate, 0)

    def wait_entries(i, carry):
        peer = partner(i)
        entry_copy(peer, peer).wait_recv()
        return carry

    lax.fori_loop(1, n, wait_entries, 0)
    listing = pltpu.make_async_copy(entry_all, entry_smem, local_sems.at[2, 0])
    listing.start()
    listing.wait()

    def split(wide):
        high = wide.astype(bf16)
        return high, (wide - high.astype(f32)).astype(bf16)

    def dot(a, b, dims):
        return lax.dot_general(a, b, (dims, ((), ())), preferred_element_type=f32)

    code_row = lax.broadcasted_iota(jnp.int32, (padded, head), 0)
    code_col = lax.broadcasted_iota(jnp.int32, (padded, head), 1)

    def encode(wide):
        size = jnp.abs(wide)
        power = jnp.ceil(jnp.log2(jnp.maximum(jnp.max(size, axis=1, keepdims=True), 1e-30)))
        root = jnp.sqrt(size * jnp.exp2(-power)) * CODE_TOP
        code = jnp.where(wide < 0.0, -root, root)
        powers = jnp.sum(jnp.where(code_row == code_col, power, 0.0), axis=0, keepdims=True)
        code = jnp.where(code_row == rows, powers, code)
        return jnp.round(code).astype(jnp.int32).astype(jnp.int16)

    def decode(code):
        wide = code.astype(jnp.int32).astype(f32)
        powers = jnp.where(code_row == code_col, wide[rows : rows + 1], 0.0)
        power = jnp.exp2(jnp.sum(powers, axis=1, keepdims=True)) * (1.0 / (CODE_TOP * CODE_TOP))
        return (wide * jnp.abs(wide) * power)[0:rows]

    def work(h, peer):
        starts = [pool_now[entry_smem[peer, 0, r]] for r in range(reqs)]
        key = block_all[h, peer, 0:padded]
        value = block_all[h, peer, padded : 2 * padded]
        query = jnp.concatenate(
            [block_all[h, peer, padded - TILE : padded], block_all[h, peer, 2 * padded - TILE : moved]],
            axis=0,
        )
        from_each = dot(query, jnp.concatenate(starts, axis=1), ((1,), (0,)))
        from_state = from_each[:, 0:head]
        for r in range(1, reqs):
            from_state = jnp.where(
                row_q % reqs == r, from_each[:, r * head : (r + 1) * head], from_state
            )
        scores = dot(query, block_all[h, peer, 0:LANES], ((1,), (1,))) * decay_pair[h]
        value_long = block_all[h, peer, padded : padded + LANES]
        attended = from_state * decay_now[h] + dot(
            jnp.concatenate(split(scores), axis=1),
            jnp.concatenate([value_long, value_long], axis=0),
            ((1,), (0,)),
        )
        att_out[h, peer] = encode(
            jnp.concatenate(
                [
                    attended[shift:TILE],
                    attended[TILE + shift : 2 * shift + rows],
                    jnp.zeros((padded - rows, head), f32),
                ],
                axis=0,
            )
        )
        value_wide = value.astype(f32)
        weighted = jnp.concatenate([value_wide * decay_tail[h, r] for r in range(reqs)], axis=1)
        added = dot(
            jnp.concatenate([key, key], axis=0),
            jnp.concatenate(split(weighted), axis=0),
            ((0,), (0,)),
        )
        fade = jnp.exp(jnp.full((8, head), -float(length), f32) * rates_ref[me * heads + h])[0:1]
        for r in range(reqs):
            staged[h, peer, r] = (
                fade * starts[r].astype(f32) + added[:, r * head : (r + 1) * head]
            ).astype(bf16)

    unroll = math.gcd(n, 4)

    def each_head(h, carry):
        def take_pool(i, inner):
            peer = partner(i)
            pool_copy(h, peer, peer).wait_recv()
            pool_now[peer] = pool_all[h, peer]
            return inner

        own_pool(h).wait()
        pool_now[me] = pool_all[h, me]
        lax.fori_loop(1, n, take_pool, 0)

        def each_group(g, inner):
            for u in range(unroll):
                i = g * unroll + u
                peer = partner(i)

                @pl.when(i > 0)
                def _():
                    block_copy(h, peer, peer).wait_recv()

            for u in range(unroll):
                work(h, partner(g * unroll + u))
            for u in range(unroll):
                i = g * unroll + u
                peer = partner(i)

                @pl.when(i > 0)
                def _():
                    att_copy(h, peer, me).start()

                @pl.when(i == 0)
                def _():
                    own_att(h).start()

                states_copy(h, peer).start()
            return inner

        lax.fori_loop(0, n // unroll, each_group, 0)
        return carry

    lax.fori_loop(0, heads, each_head, 0)

    def gather_head(h, total):
        own_att(h).wait()
        own = decode(att_in[h, me])
        att_wide[h, me] = own

        def gather(i, inner):
            peer = partner(i)
            att_copy(h, peer, peer).wait_recv()
            here = decode(att_in[h, peer])
            att_wide[h, peer] = here
            return inner + here * here

        return lax.fori_loop(1, n, gather, total + own * own)

    squares = lax.fori_loop(0, heads, gather_head, jnp.zeros((rows, head), f32))
    squares = jnp.sum(squares, axis=1, keepdims=True)
    scale = lax.rsqrt(squares * (1.0 / width) + 1e-05)

    def finish(j, carry):
        for h in range(heads):
            at = pl.ds(pl.multiple_of(j * part + h * head, head), head)
            done = att_wide[h, j] * scale * gated[:, at]
            mixed_ref[:, :, at] = done.reshape(length, reqs, head).astype(bf16)
        return carry

    lax.fori_loop(0, n, finish, 0)

    def settle(i, carry):
        peer = partner(i)
        entry_copy(peer, me).wait_send()
        for h in range(heads):
            pool_copy(h, peer, me).wait_send()
            block_copy(h, peer, me).wait_send()
            att_copy(h, peer, me).wait_send()
            states_copy(h, peer).wait()
        return carry

    lax.fori_loop(1, n, settle, 0)
    for h in range(heads):
        states_copy(h, me).wait()


def by_heads(
    n, queries, key_vectors, values, gate_logits, decay_rates, norm_gain, pool_states, pool_entry
):
    reqs, length, width = queries.shape
    head = pool_states.shape[2]
    part = width // n
    heads = part // head
    rows = reqs * length
    padded, lead, moved = plan_rows(rows)
    flat = [
        item.transpose(1, 0, 2) for item in (queries, key_vectors, values, gate_logits)
    ]
    f32, bf16 = jnp.float32, jnp.bfloat16
    vmem = pl.BlockSpec(memory_space=pltpu.VMEM)
    smem = pl.BlockSpec(memory_space=pltpu.SMEM)
    anywhere = pl.BlockSpec(memory_space=pl.ANY)
    mixed, new_states = pl.pallas_call(
        functools.partial(heads_kernel, (n, reqs, length, heads, head)),
        out_shape=(
            jax.ShapeDtypeStruct((length, reqs, width), bf16),
            jax.ShapeDtypeStruct((n * reqs, part, head), bf16),
        ),
        in_specs=[smem, smem, vmem, vmem, vmem, vmem, vmem, anywhere],
        out_specs=(vmem, anywhere),
        scratch_shapes=[
            pltpu.VMEM((heads, n, reqs, head, head), bf16),
            pltpu.VMEM((8, LANES), jnp.int32),
            pltpu.VMEM((n, 8, LANES), jnp.int32),
            pltpu.SMEM((n, 8, LANES), jnp.int32),
            pltpu.VMEM((heads, n, moved, head), bf16),
            pltpu.VMEM((heads, n, moved, head), bf16),
            pltpu.VMEM((heads, n, head, head), bf16),
            pltpu.VMEM((n, head, head), bf16),
            pltpu.VMEM((heads, n, padded, head), jnp.int16),
            pltpu.VMEM((heads, n, padded, head), jnp.int16),
            pltpu.VMEM((heads, n, rows, head), f32),
            pltpu.VMEM((rows, width), f32),
            pltpu.VMEM((heads, padded, head), f32),
            pltpu.VMEM((heads, padded, LANES), f32),
            pltpu.VMEM((heads, reqs, padded, head), f32),
            pltpu.SemaphoreType.DMA((2, n)),
            pltpu.SemaphoreType.DMA((heads, 2, n)),
            pltpu.SemaphoreType.DMA((heads, 2, n)),
            pltpu.SemaphoreType.DMA((heads, 2, n)),
            pltpu.SemaphoreType.DMA((heads, n)),
            pltpu.SemaphoreType.DMA((3, heads)),
        ],
        compiler_params=pltpu.CompilerParams(
            collective_id=0, has_side_effects=True, vmem_limit_bytes=38 * 1024 * 1024
        ),
    )(pool_entry, decay_rates, norm_gain.reshape(1, width), *flat, pool_states)
    return mixed.transpose(1, 0, 2), new_states


def on_device(
    queries, key_vectors, values, gate_logits, decay_rates, norm_gain, pool_states, pool_entry
):
    req_dev, length, feature_width = queries.shape
    head_count = decay_rates.shape[0]
    head_size = pool_states.shape[2]
    ranks = lax.axis_size("batch")
    rows = req_dev * length
    lead = -rows % TILE
    if (
        ranks > 1
        and ranks & (ranks - 1) == 0
        and feature_width % (ranks * head_size) == 0
        and pool_states.shape[0] == 1
        and head_size % LANES == 0
        and 0 < lead < min(rows, TILE)
        and rows <= LANES
        and plan_rows(rows)[0] + LANES <= plan_rows(rows)[2]
        and plan_rows(rows)[2] == 3 * plan_rows(rows)[0] - 2 * TILE
    ):
        return by_heads(
            ranks, queries, key_vectors, values, gate_logits, decay_rates, norm_gain, pool_states, pool_entry
        )
    entries = lax.all_gather(pool_entry, "batch", axis=0, tiled=True)
    spread = lax.all_to_all(pool_states, "batch", split_axis=1, concat_axis=0, tiled=True)
    chosen = jnp.take(spread, entries, axis=0)
    resumed = lax.all_to_all(chosen, "batch", split_axis=0, concat_axis=1, tiled=True)
    resumed = resumed.reshape(req_dev, head_count, head_size, head_size)
    shaped = (req_dev, length, head_count, head_size)
    attended, updated = attend(
        queries.reshape(shaped),
        key_vectors.reshape(shaped),
        values.reshape(shaped),
        resumed,
        decay_rates,
    )
    attended = attended.reshape(req_dev, length, feature_width)
    local_states = updated.astype(jnp.bfloat16).reshape(req_dev, feature_width, head_size)
    new_states = lax.all_to_all(local_states, "batch", split_axis=1, concat_axis=0, tiled=True)
    mixed = finish_output(attended, gate_logits, norm_gain)
    return (mixed, new_states)


def solution(mesh):
    placed = (
        P(("groups", "batch"), None, None),
        P(("groups", "batch"), None, None),
        P(("groups", "batch"), None, None),
        P(("groups", "batch"), None, None),
        P(),
        P(),
        P(("groups", "batch"), None, None),
        P(("groups", "batch")),
    )
    return jax.shard_map(
        on_device,
        mesh=mesh,
        in_specs=placed,
        out_specs=(P(("groups", "batch"), None, None), P("groups", "batch", None)),
        check_vma=False,
    )
```

```python
import functools
import math

import jax
import jax.numpy as jnp
from jax import lax
from jax.experimental import pallas as pl
from jax.experimental.pallas import tpu as pltpu
from jax.sharding import PartitionSpec as P


def finish_output(attended, gate_logits, norm_gain):
    mean_square = jnp.mean(attended * attended, axis=-1, keepdims=True)
    scaled = attended * lax.rsqrt(mean_square + 1e-05) * norm_gain
    return (scaled * jax.nn.sigmoid(gate_logits.astype(jnp.float32))).astype(jnp.bfloat16)


def attend(query_part, key_part, value_part, resumed, rates_here):
    length = query_part.shape[1]
    highest = lax.Precision.HIGHEST
    positions = jnp.arange(1, length + 1).astype(jnp.float32)
    decay_now = jnp.exp(-positions[:, None] * rates_here[None, :])
    from_state = jnp.einsum(
        "rtgd,rgde->rtge", query_part, resumed, preferred_element_type=jnp.float32
    )
    from_state = from_state * decay_now[None, :, :, None]
    key_wide = key_part.astype(jnp.float32)
    value_wide = value_part.astype(jnp.float32)
    distance = positions[:, None] - positions[None, :]
    decay_pair = jnp.where(
        (distance >= 0.0)[:, :, None],
        jnp.exp(-jnp.maximum(distance, 0.0)[:, :, None] * rates_here),
        0.0,
    )
    scores = (
        jnp.einsum("rtgd,rsgd->rtsg", query_part, key_part, preferred_element_type=jnp.float32)
        * decay_pair[None]
    )
    in_block = jnp.einsum("rtsg,rsge->rtge", scores, value_wide, precision=highest)
    tail_decay = jnp.exp(-(float(length) - positions)[:, None] * rates_here[None, :])
    weighted_keys = key_wide * tail_decay[None, :, :, None]
    updated = jnp.exp(-float(length) * rates_here)[None, :, None, None] * resumed.astype(
        jnp.float32
    )
    updated = updated + jnp.einsum("rsgd,rsge->rgde", weighted_keys, value_wide, precision=highest)
    return (from_state + in_block, updated)


MESH = pl.DeviceIdType.MESH
TILE = 16
LANES = 128
CODE_TOP = 32000.0


def round_up(count, unit):
    return -(-count // unit) * unit


def plan_rows(rows):
    padded = round_up(rows, TILE)
    lead = padded - rows
    moved = round_up(padded + rows + rows - lead, TILE)
    return padded, lead, moved


def heads_kernel(
    dims,
    entry_ref,
    rates_ref,
    gain_ref,
    query_ref,
    key_ref,
    value_ref,
    gate_ref,
    pool_ref,
    mixed_ref,
    new_ref,
    staged,
    entry_mine,
    entry_all,
    entry_smem,
    packed,
    block_all,
    pool_all,
    pool_now,
    att_out,
    att_in,
    att_wide,
    gated,
    decay_now,
    decay_pair,
    decay_tail,
    entry_sems,
    pool_sems,
    block_sems,
    att_sems,
    state_sems,
    local_sems,
):
    n, reqs, length, heads, head = dims
    rows = reqs * length
    padded, lead, moved = plan_rows(rows)
    part = heads * head
    width = n * part
    shift = TILE - lead
    f32, bf16 = jnp.float32, jnp.bfloat16
    me = lax.axis_index("batch")

    def partner(i):
        step = (i % 2) * (n // 2) + i // 2
        peer = 0
        bit = 1
        while bit < n:
            peer = peer + ((me // bit + step // bit) % 2) * bit
            bit *= 2
        return peer

    barrier = pltpu.get_barrier_semaphore()

    def greet(i, carry):
        pl.semaphore_signal(barrier, inc=1, device_id={"batch": partner(i)}, device_id_type=MESH)
        return carry

    lax.fori_loop(1, n, greet, 0)

    lane = lax.broadcasted_iota(jnp.int32, (8, LANES), 1)
    mine = jnp.zeros((8, LANES), jnp.int32)
    for r in range(reqs):
        mine = jnp.where(lane == r, entry_ref[r], mine)
    entry_mine[...] = mine
    entry_all[me] = mine

    def remote(src, dst, send_sem, recv_sem, peer):
        return pltpu.make_async_remote_copy(
            src_ref=src,
            dst_ref=dst,
            send_sem=send_sem,
            recv_sem=recv_sem,
            device_id={"batch": peer},
            device_id_type=MESH,
        )

    def pool_rows(h, peer):
        return pool_ref.at[0, pl.ds(pl.multiple_of(peer * part + h * head, head), head), :]

    def entry_copy(peer, slot):
        return remote(
            entry_mine, entry_all.at[slot], entry_sems.at[0, peer], entry_sems.at[1, slot], peer
        )

    def pool_copy(h, peer, slot):
        return remote(
            pool_rows(h, peer),
            pool_all.at[h, slot],
            pool_sems.at[h, 0, peer],
            pool_sems.at[h, 1, slot],
            peer,
        )

    def block_copy(h, peer, slot):
        return remote(
            packed.at[h, peer],
            block_all.at[h, slot],
            block_sems.at[h, 0, peer],
            block_sems.at[h, 1, slot],
            peer,
        )

    def att_copy(h, peer, slot):
        return remote(
            att_out.at[h, peer],
            att_in.at[h, slot],
            att_sems.at[h, 0, peer],
            att_sems.at[h, 1, slot],
            peer,
        )

    def own_pool(h):
        return pltpu.make_async_copy(pool_rows(h, me), pool_all.at[h, me], local_sems.at[0, h])

    def own_att(h):
        return pltpu.make_async_copy(att_out.at[h, me], att_in.at[h, me], local_sems.at[1, h])

    def states_copy(h, peer):
        return pltpu.make_async_copy(
            staged.at[h, peer],
            new_ref.at[
                pl.ds(peer * reqs, reqs), pl.ds(pl.multiple_of(h * head, head), head), :
            ],
            state_sems.at[h, peer],
        )

    def block_of(h, peer):
        cols = pl.ds(pl.multiple_of(peer * part + h * head, head), head)
        key, query, value = (
            ref[:, :, cols].astype(f32).reshape(rows, head) for ref in (key_ref, query_ref, value_ref)
        )
        gap = jnp.zeros((moved - 3 * rows, head), f32)
        return jnp.concatenate([key, query[:lead], value, query[lead:], gap], axis=0).astype(bf16)

    def send_pool(h):
        def body(i, carry):
            pool_copy(h, partner(i), me).start()
            return carry

        lax.fori_loop(1, n, body, 0)
        own_pool(h).start()

    def pack_block(h, peer):
        packed[h, peer] = block_of(h, peer)

    def send_block(h, ready):
        def body(i, carry):
            peer = partner(i)
            if not ready:
                pack_block(h, peer)
            block_copy(h, peer, me).start()
            return carry

        lax.fori_loop(1, n, body, 0)
        block_all[h, me] = block_of(h, me)

    def pack_first(i, carry):
        pack_block(0, partner(i))
        return carry

    lax.fori_loop(1, n, pack_first, 0)

    def send_entries(i, carry):
        entry_copy(partner(i), me).start()
        return carry

    pl.semaphore_wait(barrier, n - 1)
    lax.fori_loop(1, n, send_entries, 0)
    for h in range(heads):
        send_pool(h)
        send_block(h, h == 0)

    def time_of(index):
        return (index // reqs + 1).astype(f32)

    def query_index(shape):
        row = lax.broadcasted_iota(jnp.int32, shape, 0)
        return jnp.maximum(jnp.where(row < TILE, row - shift, row - 2 * shift), 0)

    row_q = query_index((padded, head))
    row_k = lax.broadcasted_iota(jnp.int32, (padded, head), 0)
    pair_q = query_index((padded, LANES))
    pair_k = lax.broadcasted_iota(jnp.int32, (padded, LANES), 1)
    distance = time_of(pair_q) - time_of(pair_k)
    keep = (distance >= 0.0) & (pair_q % reqs == pair_k % reqs) & (pair_k < rows)
    for h in range(heads):
        rate = rates_ref[me * heads + h]
        decay_now[h] = jnp.exp(-time_of(row_q) * rate)
        decay_pair[h] = jnp.where(keep, jnp.exp(-jnp.maximum(distance, 0.0) * rate), 0.0)
        tail = jnp.exp(-jnp.maximum(float(length) - time_of(row_k), 0.0) * rate)
        for r in range(reqs):
            decay_tail[h, r] = jnp.where((row_k < rows) & (row_k % reqs == r), tail, 0.0)

    def prepare_gate(j, carry):
        at = pl.ds(pl.multiple_of(j * part, part), part)
        gate = gate_ref[:, :, at].astype(f32).reshape(rows, part)
        gated[:, at] = gain_ref[:, at] * jax.nn.sigmoid(gate)
        return carry

    lax.fori_loop(0, n, prepare_gate, 0)

    def wait_entries(i, carry):
        peer = partner(i)
        entry_copy(peer, peer).wait_recv()
        return carry

    lax.fori_loop(1, n, wait_entries, 0)
    listing = pltpu.make_async_copy(entry_all, entry_smem, local_sems.at[2, 0])
    listing.start()
    listing.wait()

    def split(wide):
        high = wide.astype(bf16)
        return high, (wide - high.astype(f32)).astype(bf16)

    def dot(a, b, dims):
        return lax.dot_general(a, b, (dims, ((), ())), preferred_element_type=f32)

    code_row = lax.broadcasted_iota(jnp.int32, (padded, head), 0)
    code_col = lax.broadcasted_iota(jnp.int32, (padded, head), 1)

    def encode(wide):
        size = jnp.abs(wide)
        power = jnp.ceil(jnp.log2(jnp.maximum(jnp.max(size, axis=1, keepdims=True), 1e-30)))
        root = jnp.sqrt(size * jnp.exp2(-power)) * CODE_TOP
        code = jnp.where(wide < 0.0, -root, root)
        powers = jnp.sum(jnp.where(code_row == code_col, power, 0.0), axis=0, keepdims=True)
        code = jnp.where(code_row == rows, powers, code)
        return jnp.round(code).astype(jnp.int32).astype(jnp.int16)

    def decode(code):
        wide = code.astype(jnp.int32).astype(f32)
        powers = jnp.where(code_row == code_col, wide[rows : rows + 1], 0.0)
        power = jnp.exp2(jnp.sum(powers, axis=1, keepdims=True)) * (1.0 / (CODE_TOP * CODE_TOP))
        return (wide * jnp.abs(wide) * power)[0:rows]

    def work(h, peer):
        starts = [pool_now[entry_smem[peer, 0, r]] for r in range(reqs)]
        key = block_all[h, peer, 0:padded]
        value = block_all[h, peer, padded : 2 * padded]
        query = jnp.concatenate(
            [block_all[h, peer, padded - TILE : padded], block_all[h, peer, 2 * padded - TILE : moved]],
            axis=0,
        )
        from_each = dot(query, jnp.concatenate(starts, axis=1), ((1,), (0,)))
        from_state = from_each[:, 0:head]
        for r in range(1, reqs):
            from_state = jnp.where(
                row_q % reqs == r, from_each[:, r * head : (r + 1) * head], from_state
            )
        scores = dot(query, block_all[h, peer, 0:LANES], ((1,), (1,))) * decay_pair[h]
        value_long = block_all[h, peer, padded : padded + LANES]
        attended = from_state * decay_now[h] + dot(
            jnp.concatenate(split(scores), axis=1),
            jnp.concatenate([value_long, value_long], axis=0),
            ((1,), (0,)),
        )
        att_out[h, peer] = encode(
            jnp.concatenate(
                [
                    attended[shift:TILE],
                    attended[TILE + shift : 2 * shift + rows],
                    jnp.zeros((padded - rows, head), f32),
                ],
                axis=0,
            )
        )
        value_wide = value.astype(f32)
        weighted = jnp.concatenate([value_wide * decay_tail[h, r] for r in range(reqs)], axis=1)
        added = dot(
            jnp.concatenate([key, key], axis=0),
            jnp.concatenate(split(weighted), axis=0),
            ((0,), (0,)),
        )
        fade = jnp.exp(jnp.full((8, head), -float(length), f32) * rates_ref[me * heads + h])[0:1]
        for r in range(reqs):
            staged[h, peer, r] = (
                fade * starts[r].astype(f32) + added[:, r * head : (r + 1) * head]
            ).astype(bf16)

    def gather_head(h, total):
        own_att(h).wait()
        own = decode(att_in[h, me])
        att_wide[h, me] = own

        def gather(i, inner):
            peer = partner(i)
            att_copy(h, peer, peer).wait_recv()
            here = decode(att_in[h, peer])
            att_wide[h, peer] = here
            return inner + here * here

        return lax.fori_loop(1, n, gather, total + own * own)

    lag = min(2, heads)
    unroll = math.gcd(n, 4)

    def each_head(h, carry):
        def take_pool(i, inner):
            peer = partner(i)
            pool_copy(h, peer, peer).wait_recv()
            pool_now[peer] = pool_all[h, peer]
            return inner

        own_pool(h).wait()
        pool_now[me] = pool_all[h, me]
        lax.fori_loop(1, n, take_pool, 0)

        def each_group(g, inner):
            for u in range(unroll):
                i = g * unroll + u
                peer = partner(i)

                @pl.when(i > 0)
                def _():
                    block_copy(h, peer, peer).wait_recv()

            for u in range(unroll):
                work(h, partner(g * unroll + u))
            for u in range(unroll):
                i = g * unroll + u
                peer = partner(i)

                @pl.when(i > 0)
                def _():
                    att_copy(h, peer, me).start()

                @pl.when(i == 0)
                def _():
                    own_att(h).start()

                states_copy(h, peer).start()
            return inner

        lax.fori_loop(0, n // unroll, each_group, 0)
        return lax.cond(h >= lag, lambda total: gather_head(h - lag, total), lambda total: total, carry)

    squares = lax.fori_loop(0, heads, each_head, jnp.zeros((rows, head), f32))

    squares = lax.fori_loop(heads - lag, heads, gather_head, squares)
    squares = jnp.sum(squares, axis=1, keepdims=True)
    scale = lax.rsqrt(squares * (1.0 / width) + 1e-05)

    def finish(j, carry):
        for h in range(heads):
            at = pl.ds(pl.multiple_of(j * part + h * head, head), head)
            done = att_wide[h, j] * scale * gated[:, at]
            mixed_ref[:, :, at] = done.reshape(length, reqs, head).astype(bf16)
        return carry

    lax.fori_loop(0, n, finish, 0)

    def settle(i, carry):
        peer = partner(i)
        entry_copy(peer, me).wait_send()
        for h in range(heads):
            pool_copy(h, peer, me).wait_send()
            block_copy(h, peer, me).wait_send()
            att_copy(h, peer, me).wait_send()
            states_copy(h, peer).wait()
        return carry

    lax.fori_loop(1, n, settle, 0)
    for h in range(heads):
        states_copy(h, me).wait()


def by_heads(
    n, queries, key_vectors, values, gate_logits, decay_rates, norm_gain, pool_states, pool_entry
):
    reqs, length, width = queries.shape
    head = pool_states.shape[2]
    part = width // n
    heads = part // head
    rows = reqs * length
    padded, lead, moved = plan_rows(rows)
    flat = [
        item.transpose(1, 0, 2) for item in (queries, key_vectors, values, gate_logits)
    ]
    f32, bf16 = jnp.float32, jnp.bfloat16
    vmem = pl.BlockSpec(memory_space=pltpu.VMEM)
    smem = pl.BlockSpec(memory_space=pltpu.SMEM)
    anywhere = pl.BlockSpec(memory_space=pl.ANY)
    mixed, new_states = pl.pallas_call(
        functools.partial(heads_kernel, (n, reqs, length, heads, head)),
        out_shape=(
            jax.ShapeDtypeStruct((length, reqs, width), bf16),
            jax.ShapeDtypeStruct((n * reqs, part, head), bf16),
        ),
        in_specs=[smem, smem, vmem, vmem, vmem, vmem, vmem, anywhere],
        out_specs=(vmem, anywhere),
        scratch_shapes=[
            pltpu.VMEM((heads, n, reqs, head, head), bf16),
            pltpu.VMEM((8, LANES), jnp.int32),
            pltpu.VMEM((n, 8, LANES), jnp.int32),
            pltpu.SMEM((n, 8, LANES), jnp.int32),
            pltpu.VMEM((heads, n, moved, head), bf16),
            pltpu.VMEM((heads, n, moved, head), bf16),
            pltpu.VMEM((heads, n, head, head), bf16),
            pltpu.VMEM((n, head, head), bf16),
            pltpu.VMEM((heads, n, padded, head), jnp.int16),
            pltpu.VMEM((heads, n, padded, head), jnp.int16),
            pltpu.VMEM((heads, n, rows, head), f32),
            pltpu.VMEM((rows, width), f32),
            pltpu.VMEM((heads, padded, head), f32),
            pltpu.VMEM((heads, padded, LANES), f32),
            pltpu.VMEM((heads, reqs, padded, head), f32),
            pltpu.SemaphoreType.DMA((2, n)),
            pltpu.SemaphoreType.DMA((heads, 2, n)),
            pltpu.SemaphoreType.DMA((heads, 2, n)),
            pltpu.SemaphoreType.DMA((heads, 2, n)),
            pltpu.SemaphoreType.DMA((heads, n)),
            pltpu.SemaphoreType.DMA((3, heads)),
        ],
        compiler_params=pltpu.CompilerParams(
            collective_id=0, has_side_effects=True, vmem_limit_bytes=38 * 1024 * 1024
        ),
    )(pool_entry, decay_rates, norm_gain.reshape(1, width), *flat, pool_states)
    return mixed.transpose(1, 0, 2), new_states


def on_device(
    queries, key_vectors, values, gate_logits, decay_rates, norm_gain, pool_states, pool_entry
):
    req_dev, length, feature_width = queries.shape
    head_count = decay_rates.shape[0]
    head_size = pool_states.shape[2]
    ranks = lax.axis_size("batch")
    rows = req_dev * length
    lead = -rows % TILE
    if (
        ranks > 1
        and ranks & (ranks - 1) == 0
        and feature_width % (ranks * head_size) == 0
        and pool_states.shape[0] == 1
        and head_size % LANES == 0
        and 0 < lead < min(rows, TILE)
        and rows <= LANES
        and plan_rows(rows)[0] + LANES <= plan_rows(rows)[2]
        and plan_rows(rows)[2] == 3 * plan_rows(rows)[0] - 2 * TILE
    ):
        return by_heads(
            ranks, queries, key_vectors, values, gate_logits, decay_rates, norm_gain, pool_states, pool_entry
        )
    entries = lax.all_gather(pool_entry, "batch", axis=0, tiled=True)
    spread = lax.all_to_all(pool_states, "batch", split_axis=1, concat_axis=0, tiled=True)
    chosen = jnp.take(spread, entries, axis=0)
    resumed = lax.all_to_all(chosen, "batch", split_axis=0, concat_axis=1, tiled=True)
    resumed = resumed.reshape(req_dev, head_count, head_size, head_size)
    shaped = (req_dev, length, head_count, head_size)
    attended, updated = attend(
        queries.reshape(shaped),
        key_vectors.reshape(shaped),
        values.reshape(shaped),
        resumed,
        decay_rates,
    )
    attended = attended.reshape(req_dev, length, feature_width)
    local_states = updated.astype(jnp.bfloat16).reshape(req_dev, feature_width, head_size)
    new_states = lax.all_to_all(local_states, "batch", split_axis=1, concat_axis=0, tiled=True)
    mixed = finish_output(attended, gate_logits, norm_gain)
    return (mixed, new_states)


def solution(mesh):
    placed = (
        P(("groups", "batch"), None, None),
        P(("groups", "batch"), None, None),
        P(("groups", "batch"), None, None),
        P(("groups", "batch"), None, None),
        P(),
        P(),
        P(("groups", "batch"), None, None),
        P(("groups", "batch")),
    )
    return jax.shard_map(
        on_device,
        mesh=mesh,
        in_specs=placed,
        out_specs=(P(("groups", "batch"), None, None), P("groups", "batch", None)),
        check_vma=False,
    )
```
